128 devices in a mesh: gx: 8 (over z_hi, y), gy: 16 (over z_lo, x, core).
Axes of the slice: x: 4, y: 4, z: 4 (z_hi: 2, z_lo: 2; z = z_hi * 2 + z_lo), core: 2. Of those that a mesh axis runs over, the one named last changes fastest.
Arguments:
- tokens: bfloat16 [1024, 16384], P('gy', 'gx'), may hold values from -6 to 6
- gate_weight: bfloat16 [16384, 26624], P('gx', 'gy'), may hold values from -0.046875 to 0.046875
- up_weight: bfloat16 [16384, 26624], P('gx', 'gy'), may hold values from -0.046875 to 0.046875
- gate_scale: float32 [26624], P('gy'), may hold values from 0.5 to 2
- up_scale: float32 [26624], P('gy'), may hold values from 0.5 to 2
- down_weight: bfloat16 [26624, 16384], P('gy', 'gx'), may hold values from -0.0390625 to 0.0390625
- down_scale: float32 [16384], P('gx'), may hold values from 0.5 to 2
Outputs:
- mixed: bfloat16 [1024, 16384], P('gy', 'gx')
The draws below stay inside these ranges and needn't reach their ends.
All inputs are finite; a program needn't handle non-finite values.
Results may differ from the reference program's by a relative error of at most 0.005.
Values may be sent and summed in bfloat16 or wider, within the bound.
A program may use at most 128 MiB of HBM per device.

```python
import math
import jax
import jax.numpy as jnp

D = 16384
FF = 26624
B = 1024


def steps_of(key, dims, pieces, smallest, high):
    level = 1.0
    for position, parts in pieces:
        heights = jax.random.uniform(jax.random.fold_in(jax.random.fold_in(key, 6), position), (parts,), jnp.float32, smallest / len(pieces), high / len(pieces))
        level = level * jnp.repeat(jnp.exp(heights), dims[position] // parts).reshape((-1,) + (1,) * (len(dims) - 1 - position))
    return level


def centred(key, extent, scale, reach, split=(), kind=jnp.bfloat16):
    factor_of = steps_of(key, extent, split, -0.22, 0.18) if split else 1.0
    values = jax.random.normal(key, extent, jnp.float32) * scale * factor_of
    return jnp.minimum(jnp.maximum(values, -reach), reach).astype(kind)


def setup_inputs(seed: int = 0) -> dict:
    key_list = jax.random.split(jax.random.key(seed), 8)
    tokens = centred(key_list[0], (B, D), 1.0, 6.0, ((0, 16), (1, 8)))
    gate_weight = centred(key_list[1], (D, FF), D ** -0.5, 0.046875, ((0, 8), (1, 16)))
    up_weight = centred(key_list[2], (D, FF), D ** -0.5, 0.046875, ((0, 8), (1, 16)))
    gate_scale = jnp.clip(jnp.exp(math.log(2.0) - 1.3862944 * jax.random.uniform(key_list[3], (FF,), jnp.float32) ** steps_of(key_list[3], (FF,), ((0, 16),), -0.2, 0.2)), 0.5, 2.0)
    up_scale = jnp.clip(jnp.exp(math.log(2.0) - 1.3862944 * jax.random.uniform(key_list[4], (FF,), jnp.float32) ** steps_of(key_list[4], (FF,), ((0, 16),), -0.2, 0.2)), 0.5, 2.0)
    down_weight = centred(key_list[5], (FF, D), FF ** -0.5, 0.0390625, ((0, 16), (1, 8)))
    down_scale = jnp.clip(jnp.exp(math.log(2.0) - 1.3862944 * jax.random.uniform(key_list[6], (D,), jnp.float32) ** steps_of(key_list[6], (D,), ((0, 8),), -0.2, 0.2)), 0.5, 2.0)
    return dict(tokens=tokens, gate_weight=gate_weight, up_weight=up_weight, gate_scale=gate_scale, up_scale=up_scale, down_weight=down_weight, down_scale=down_scale)


def reference(tokens, gate_weight, up_weight, gate_scale, up_scale, down_weight, down_scale):
    gate_sum = jnp.dot(tokens, gate_weight, preferred_element_type=jnp.float32)
    up_sum = jnp.dot(tokens, up_weight, preferred_element_type=jnp.float32)
    gate = gate_sum * gate_scale[None, :]
    up_value = up_sum * up_scale[None, :]
    hidden = (jax.nn.silu(gate) * up_value).astype(jnp.bfloat16)
    product = jnp.dot(hidden, down_weight, preferred_element_type=jnp.float32)
    return (product * down_scale[None, :]).astype(jnp.bfloat16)
```

```python
import jax
import jax.numpy as jnp
from jax import lax
from jax.experimental import pallas as pl
from jax.experimental.pallas import tpu as pltpu
from jax.sharding import PartitionSpec as P

MESH = pl.DeviceIdType.MESH
BF, F32 = jnp.bfloat16, jnp.float32
NC = 8
K, N, N2, M = 2048, 1664, 3328, 2048
HALF = 896
LIFT = 2.0**50
TINY = 1e-37

S1P, S1M, S2P, S2M, S3P, S3M, ZS, HYP, HYM, HRP, HRM, HZ0, HZ1, HZ2, HZ3, CRS, XSN, TKF = range(18)
PER = 18
TOK = NC * PER
TK_CORE, TK_Z, TK_X, TK_ZX, ZLS = TOK, TOK + 1, TOK + 2, TOK + 5, TOK + 8
NSEM = TOK + 9

PIECES = ((0, 0, 1024, 0), (0, 1024, 640, 1024), (1, 0, 384, 1664), (1, 384, 1024, 2048), (1, 1408, 256, 3072))
W_FOR_TILE = ((0,), (1, 2), (3,), (4,))


def encode(v):
    v = v * LIFT
    return (v * jnp.abs(v)).astype(BF)


def decode(q):
    q = q.astype(F32)
    return q * lax.rsqrt(jnp.maximum(jnp.abs(q), TINY))


def recode(s):
    return (s * jnp.abs(s)).astype(BF)


def body(tok, wg, wu, gs, us, wd, ds, out, W, WD, T, PT, RL, RM, RP, ZR, H, D, CR, XS, XR, ACC, ZLB, ZLR, ssem, rsem, lsem):
    gx, gy = lax.axis_index("gx"), lax.axis_index("gy")
    zh, y = gx // 4, lax.rem(gx, 4)
    zl, x, core = gy // 8, lax.rem(gy // 2, 4), lax.rem(gy, 2)
    zo, other = 1 - zh, 1 - core
    yp, ym, y2 = lax.rem(y + 1, 4), lax.rem(y + 3, 4), lax.rem(y + 2, 4)

    def at(zh_=zh, y_=y, zl_=zl, x_=x, core_=core):
        return (zh_ * 4 + y_, zl_ * 8 + x_ * 2 + core_)

    to_yp, to_ym, to_zh, to_zl, to_core = at(y_=yp), at(y_=ym), at(zh_=zo), at(zl_=1 - zl), at(core_=other)
    xd = [lax.rem(x + d, 4) for d in range(4)]

    def own(y_, z_):
        return y_ * 2 + z_

    def copy(src, dst, k, to):
        return pltpu.make_async_remote_copy(
            src_ref=src, dst_ref=dst, send_sem=ssem.at[k], recv_sem=rsem.at[k], device_id=to, device_id_type=MESH
        )

    def arrived(dst, k):
        copy(dst, dst, k, to_core).wait_recv()

    def sent(src, k):
        copy(src, src, k, to_core).wait_send()

    w_copies = [
        pltpu.make_async_copy(
            (wg, wu)[m].at[:, pl.ds(c0, n)], W.at[:, pl.ds(d0, n)], lsem.at[i]
        )
        for i, (m, c0, n, d0) in enumerate(PIECES)
    ]
    own_copy = pltpu.make_async_copy(tok, T.at[0, core], lsem.at[5])
    wd_copy = pltpu.make_async_copy(wd, WD, lsem.at[6])
    own_copy.start()
    for c in w_copies:
        c.start()
    wd_copy.start()

    barrier = pltpu.get_barrier_semaphore()
    partners = [to_yp, to_ym, to_zh, to_zl, to_core] + [at(x_=xd[d]) for d in (1, 2, 3)]
    for p in partners:
        pl.semaphore_signal(barrier, inc=1, device_id=p, device_id_type=MESH)
    pl.semaphore_wait(barrier, len(partners))

    CHUNK = {(0, 0): 0, (0, 1): 1, (1, 1): 2, (3, 1): 3, (2, 1): 4, (2, 0): 5, (1, 0): 6, (3, 0): 7}

    def dx_of(c):
        return jnp.where((c == 2) | (c == 6), 1, jnp.where((c == 3) | (c == 7), 3, 2))

    copy(tok, T.at[0, core], TK_CORE, to_core).start()
    copy(tok, T.at[1, core], TK_Z, to_zl).start()
    for d in (2, 1, 3):
        copy(tok, T.at[CHUNK[((4 - d) % 4, 0)], core], TK_X + d - 1, at(x_=xd[d])).start()

    def recv_index(c):
        d = 4 - dx_of(c)
        return jnp.where(c == 1, TK_Z, jnp.where(c < 5, TK_ZX, TK_X) + d - 1)

    def forward_tokens(c):
        arrived(T.at[c, core], recv_index(c))
        copy(T.at[c, core], T.at[c, core], c * PER + TKF, to_core).start()

        @pl.when(c == 1)
        def _():
            for d in (1, 3, 2):
                copy(
                    T.at[1, core], T.at[CHUNK[((4 - d) % 4, 1)], core], TK_ZX + d - 1, at(x_=xd[d])
                ).start()

    def gate_up(c):
        @pl.when(c == 0)
        def _():
            own_copy.wait()
            arrived(T.at[0, other], TK_CORE)

        @pl.when(c > 0)
        def _():
            arrived(T.at[c, other], c * PER + TKF)

        def tile(n0, width):
            rows = T[c].reshape(128, K)
            part = jnp.dot(rows, W[:, pl.ds(n0, width)], preferred_element_type=F32)
            PT[c, :, :, pl.ds(n0, width)] = encode(part).reshape(8, 16, width)

        def step(n, carry):
            @pl.when(c == 0)
            def _():
                for t in range(3):

                    @pl.when(n == t)
                    def _():
                        for i in W_FOR_TILE[t]:
                            w_copies[i].wait()

            tile(pl.multiple_of(n * 1024, 1024), 1024)
            return carry

        lax.fori_loop(0, 3, step, 0)

        @pl.when(c == 0)
        def _():
            w_copies[4].wait()

        tile(3072, 256)
        b = c * PER
        copy(PT.at[c, own(y2, 0)], RL.at[c, 0], b + S1P, to_yp).start()
        copy(PT.at[c, own(y2, 1)], RL.at[c, 1], b + S1M, to_ym).start()
        copy(PT.at[c, own(yp, 1)], RM.at[c, 1], b + S2P, to_yp).start()
        copy(PT.at[c, own(ym, 0)], RP.at[c, 0], b + S2M, to_ym).start()

    def relay(c):
        b = c * PER
        arrived(RL.at[c, 0], b + S1P)
        o = own(yp, 0)
        PT[c, o] = recode(decode(PT[c, o]) + decode(RL[c, 0]))
        copy(PT.at[c, o], RM.at[c, 0], b + S3P, to_yp).start()
        arrived(RL.at[c, 1], b + S1M)
        o = own(ym, 1)
        PT[c, o] = recode(decode(PT[c, o]) + decode(RL[c, 1]))
        copy(PT.at[c, o], RP.at[c, 1], b + S3M, to_ym).start()

    def over_y(c):
        b = c * PER
        arrived(RM.at[c, 1], b + S2P)
        arrived(RP.at[c, 0], b + S2M)
        arrived(RM.at[c, 0], b + S3P)
        arrived(RP.at[c, 1], b + S3M)
        o = own(y, zo)
        PT[c, o] = recode(decode(PT[c, o]) + decode(RM[c, zo]) + decode(RP[c, zo]))
        copy(PT.at[c, o], ZR.at[c], b + ZS, to_zh).start()

    def hidden_rows(c):
        b = c * PER
        arrived(ZR.at[c], b + ZS)
        o = own(y, zh)

        def total(cols):
            return (
                decode(PT[c, o, :, cols]) + decode(RM[c, zh, :, cols])
                + decode(RP[c, zh, :, cols]) + decode(ZR[c, :, cols])
            )

        gate = total(pl.ds(0, N)) * (gs[...] * (1.0 / LIFT))[None, :]
        up = total(pl.ds(N, N)) * (us[...] * (1.0 / LIFT))[None, :]
        H[c, o] = (jax.nn.silu(gate) * up).astype(BF)
        copy(H.at[c, o], H.at[c, o], b + HYP, to_yp).start()
        copy(H.at[c, o], H.at[c, o], b + HYM, to_ym).start()
        copy(H.at[c, o], H.at[c, o], b + HZ0, to_zh).start()

    def near_rows(c):
        b = c * PER
        om, op = own(ym, zh), own(yp, zh)
        arrived(H.at[c, om], b + HYP)
        left = H.at[c, om, :, pl.ds(0, HALF)]
        copy(left, left, b + HRP, to_yp).start()
        copy(H.at[c, om], H.at[c, om], b + HZ1, to_zh).start()
        arrived(H.at[c, op], b + HYM)
        right = H.at[c, op, :, pl.ds(HALF, N - HALF)]
        copy(right, right, b + HRM, to_ym).start()
        copy(H.at[c, op], H.at[c, op], b + HZ2, to_zh).start()

    def far_rows(c):
        b = c * PER
        o = own(y2, zh)
        arrived(H.at[c, o, :, pl.ds(0, HALF)], b + HRP)
        arrived(H.at[c, o, :, pl.ds(HALF, N - HALF)], b + HRM)
        copy(H.at[c, o], H.at[c, o], b + HZ3, to_zh).start()

    def down(c):
        b = c * PER
        arrived(H.at[c, own(y, zo)], b + HZ0)
        arrived(H.at[c, own(ym, zo)], b + HZ1)
        arrived(H.at[c, own(yp, zo)], b + HZ2)
        arrived(H.at[c, own(y2, zo)], b + HZ3)
        slot = lax.rem(c, 2)

        @pl.when(c == 0)
        def _():
            wd_copy.wait()

        @pl.when(c >= 2)
        def _():
            sent(D.at[slot, other], (c - 2) * PER + CRS)

        def step(n, carry):
            cols = pl.ds(pl.multiple_of(n * 1024, 1024), 1024)
            rows = H[c].reshape(128, N)
            D[slot, :, :, cols] = jnp.dot(rows, WD[:, cols], preferred_element_type=F32).reshape(2, 64, 1024)
            return carry

        lax.fori_loop(0, 2, step, 0)
        copy(D.at[slot, other], CR.at[c], b + CRS, to_core).start()

    def over_core(c):
        b = c * PER
        slot = lax.rem(c, 2)
        arrived(CR.at[c], b + CRS)

        @pl.when(c < 2)
        def _():
            ACC[c] = D[slot, core] + CR[c]

        @pl.when(c >= 2)
        def _():
            XS[c - 2] = (D[slot, core] + CR[c]).astype(BF)
            copy(XS.at[c - 2], XR.at[c - 2], b + XSN, at(x_=lax.rem(x + dx_of(c), 4))).start()

    def over_x(first, a):
        for c in range(first, first + 3):
            arrived(XR.at[c - 2], c * PER + XSN)
        return ACC[a] + (XR[first - 2].astype(F32) + XR[first - 1].astype(F32) + XR[first].astype(F32))

    def for_partner():
        ZLB[...] = over_x(2, 1).astype(BF)
        copy(ZLB, ZLR, ZLS, to_zl).start()

    plan = (
        (gate_up, 0),
        (forward_tokens, -1),
        (hidden_rows, 2),
        (far_rows, 3),
        (over_y, 1),
        (down, 4),
        (over_core, 5),
        (near_rows, 2),
        (relay, 0),
    )

    def step(s, carry):
        for task, lag in plan:
            c = s - lag

            @pl.when((c >= (1 if task is forward_tokens else 0)) & (c < NC))
            def _():
                task(c)

            if task is down:

                @pl.when(s == 11)
                def _():
                    for_partner()

        return carry

    lax.fori_loop(0, NC + 5, step, 0)

    near = over_x(5, 0)
    arrived(ZLR, ZLS)
    out[...] = ((near + ZLR[...].astype(F32)) * ds[...][None, :]).astype(BF)

    def drain(c, carry):
        b = c * PER
        for k in (S1P, S1M, S2P, S2M, S3P, S3M, ZS):
            sent(PT.at[c, 0], b + k)
        for k in (HYP, HYM, HZ0, HZ1, HZ2, HZ3):
            sent(H.at[c, 0], b + k)
        sent(H.at[c, 0, :, pl.ds(0, HALF)], b + HRP)
        sent(H.at[c, 0, :, pl.ds(HALF, N - HALF)], b + HRM)

        @pl.when(c >= NC - 2)
        def _():
            sent(D.at[0, 0], b + CRS)

        @pl.when(c >= 2)
        def _():
            sent(XS.at[0], b + XSN)

        @pl.when(c >= 1)
        def _():
            sent(T.at[c, core], b + TKF)

        return carry

    lax.fori_loop(0, NC, drain, 0)
    for k in range(TK_CORE, TK_CORE + 8):
        sent(T.at[0, core], k)
    sent(ZLB, ZLS)


def on_device(tokens, gate_weight, up_weight, gate_scale, up_scale, down_weight, down_scale):
    hbm, vmem = pl.BlockSpec(memory_space=pl.ANY), pl.BlockSpec(memory_space=pltpu.VMEM)
    return pl.pallas_call(
        body,
        name="gated_layer",
        out_shape=jax.ShapeDtypeStruct((64, M), BF),
        in_specs=[hbm, hbm, hbm, vmem, vmem, hbm, vmem],
        out_specs=vmem,
        scratch_shapes=[
            pltpu.VMEM((K, N2), BF),
            pltpu.VMEM((N, M), BF),
            pltpu.VMEM((NC, 2, 64, K), BF),
            pltpu.VMEM((NC, 8, 16, N2), BF),
            pltpu.VMEM((NC, 2, 16, N2), BF),
            pltpu.VMEM((NC, 2, 16, N2), BF),
            pltpu.VMEM((NC, 2, 16, N2), BF),
            pltpu.VMEM((NC, 16, N2), BF),
            pltpu.VMEM((NC, 8, 16, N), BF),
            pltpu.VMEM((2, 2, 64, M), F32),
            pltpu.VMEM((NC, 64, M), F32),
            pltpu.VMEM((6, 64, M), BF),
            pltpu.VMEM((6, 64, M), BF),
            pltpu.VMEM((2, 64, M), F32),
            pltpu.VMEM((64, M), BF),
            pltpu.VMEM((64, M), BF),
            pltpu.SemaphoreType.DMA((NSEM,)),
            pltpu.SemaphoreType.DMA((NSEM,)),
            pltpu.SemaphoreType.DMA((7,)),
        ],
        compiler_params=pltpu.CompilerParams(
            collective_id=0, has_side_effects=True, vmem_limit_bytes=62 * 2**20
        ),
        cost_estimate=pl.CostEstimate(
            flops=2 * 1024 * K * N2 + 2 * 1024 * N * M, bytes_accessed=2 * (K * N2 + N * M), transcendentals=0
        ),
    )(tokens, gate_weight, up_weight, gate_scale, up_scale, down_weight, down_scale)


def solution(mesh):
    return jax.shard_map(
        on_device,
        mesh=mesh,
        in_specs=(
            P("gy", "gx"),
            P("gx", "gy"),
            P("gx", "gy"),
            P("gy"),
            P("gy"),
            P("gy", "gx"),
            P("gx"),
        ),
        out_specs=P("gy", "gx"),
        check_vma=False,
    )
```

```python
import jax
import jax.numpy as jnp
from jax import lax
from jax.experimental import pallas as pl
from jax.experimental.pallas import tpu as pltpu
from jax.sharding import PartitionSpec as P

MESH = pl.DeviceIdType.MESH
BF, F32 = jnp.bfloat16, jnp.float32
NC = 8
K, N, N2, M = 2048, 1664, 3328, 2048
HALF = 896
LIFT = 2.0**50
TINY = 1e-37

CHUNKS = ("own", "x2", "z", "zx2", "zx1", "zx3", "mixA", "mixB")
DIRECT = (7,)
SPLIT = (7,)
ORDER = (
    ("send_far", 0), ("gate_up", 0), ("forward", 1), ("forward", 2), ("relay", 0), ("gate_up", 1), ("gate_up", 2),
    ("forward", 4), ("send_near", 0), ("over_y", 0), ("relay", 1), ("forward", 3), ("hidden", 0), ("relay", 2),
    ("forward", 5), ("forward", 6), ("gate_up", 3), ("over_y", 1), ("near", 0), ("hidden", 1), ("over_y", 2),
    ("relay", 3), ("gate_up", 4), ("far", 0), ("hidden", 2), ("near", 1), ("over_y", 3), ("gate_up", 5), ("far", 1),
    ("down", 0), ("forward", 7), ("relay", 5), ("relay", 4), ("hidden", 3), ("near", 2), ("gate_up", 6),
    ("over_y", 5), ("down", 1), ("over_y", 4), ("near", 3), ("far", 2), ("relay", 6), ("hidden", 5), ("hidden", 4),
    ("gate_up", 7), ("far", 3), ("over_core", 1), ("over_y", 6), ("near", 4), ("over_core", 0), ("near", 5),
    ("down", 2), ("relay", 7), ("down", 3), ("far", 4), ("far", 5), ("hidden", 6), ("over_core", 2), ("over_core", 3),
    ("over_y", 7), ("down", 4), ("down", 5), ("near", 6), ("far", 6), ("over_core", 4), ("over_core", 5),
    ("hidden", 7), ("down", 6), ("over_core", 6), ("partner", 0), ("down_a", 7), ("down_b", 7), ("over_core_a", 7),
    ("over_core_b", 7),
)

ALONG_X = {"x2": (2,), "zx1": (1,), "zx2": (2,), "zx3": (3,), "mixA": (1, 3), "mixB": (1, 3)}
PIECES = ((0, 0, 1024, 0), (0, 1024, 640, 1024), (1, 0, 384, 1664), (1, 384, 1024, 2048), (1, 1408, 256, 3072))
W_FOR_TILE = ((0,), (1, 2), (3,), (4,))
NSEM = 176


def encode(v):
    v = v * LIFT
    return (v * jnp.abs(v)).astype(BF)


def decode(q):
    q = q.astype(F32)
    return q * lax.rsqrt(jnp.maximum(jnp.abs(q), TINY))


def recode(s):
    return (s * jnp.abs(s)).astype(BF)


def body(tok, wg, wu, gs, us, wd, ds, out, W, WD, T, PT, RL, RM, RP, ZR, H, D, CR, XS, XR, ACC, ZLB, ZLR, ssem, rsem, lsem):
    gx, gy = lax.axis_index("gx"), lax.axis_index("gy")
    zh, y = gx // 4, lax.rem(gx, 4)
    zl, x, core = gy // 8, lax.rem(gy // 2, 4), lax.rem(gy, 2)
    zo, other = 1 - zh, 1 - core
    yp, ym, y2 = lax.rem(y + 1, 4), lax.rem(y + 3, 4), lax.rem(y + 2, 4)

    def at(zh_=zh, y_=y, zl_=zl, x_=x, core_=core):
        return (zh_ * 4 + y_, zl_ * 8 + x_ * 2 + core_)

    to_yp, to_ym, to_y2 = at(y_=yp), at(y_=ym), at(y_=y2)
    to_zh, to_zh_yp, to_zh_ym, to_zh_y2 = at(zh_=zo), at(zh_=zo, y_=yp), at(zh_=zo, y_=ym), at(zh_=zo, y_=y2)
    to_zl, to_core = at(zl_=1 - zl), at(core_=other)
    to_x = [None] + [at(x_=lax.rem(x + d, 4)) for d in (1, 2, 3)]

    def own(y_, z_):
        return y_ * 2 + z_

    semaphore, on_way = {}, {}

    def copy(src, dst, key, to):
        k = semaphore.setdefault(key, len(semaphore))
        return pltpu.make_async_remote_copy(
            src_ref=src, dst_ref=dst, send_sem=ssem.at[k], recv_sem=rsem.at[k], device_id=to, device_id_type=MESH
        )

    def send(src, dst, key, to):
        on_way[key] = copy(src, dst, key, to)
        on_way[key].start()

    def arrived(dst, key):
        copy(dst, dst, key, to_core).wait_recv()

    w_copies = [
        pltpu.make_async_copy((wg, wu)[m].at[:, pl.ds(c0, n)], W.at[:, pl.ds(d0, n)], lsem.at[i])
        for i, (m, c0, n, d0) in enumerate(PIECES)
    ]
    own_copy = pltpu.make_async_copy(tok, T.at[CHUNKS.index("own"), core], lsem.at[5])
    wd_copy = pltpu.make_async_copy(wd, WD, lsem.at[6])
    own_copy.start()
    for c in w_copies:
        c.start()

    barrier = pltpu.get_barrier_semaphore()
    partners = [to_yp, to_ym, to_y2, to_zh, to_zh_yp, to_zh_ym, to_zh_y2, to_zl, to_core] + to_x[1:]
    for p in partners:
        pl.semaphore_signal(barrier, inc=1, device_id=p, device_id_type=MESH)
    pl.semaphore_wait(barrier, len(partners))

    def chunk_tokens(c):
        name = CHUNKS[c]
        if name[:3] == "mix":
            return [(T.at[c, core, pl.ds(32 * i, 32)], ("tok", name, d)) for i, d in enumerate((1, 3))]
        return [(T.at[c, core], ("tok", name))]

    def send_far(_):
        send(tok, T.at[CHUNKS.index("x2"), core], ("tok", "x2"), to_x[2])

    def send_near(_):
        for i, name in enumerate(("mixA", "mixB")):
            c = CHUNKS.index(name)
            rows = tok.at[pl.ds(32 * i, 32)]
            send(rows, T.at[c, core, pl.ds(32, 32)], ("tok", name, 3), to_x[1])
            send(rows, T.at[c, core, pl.ds(0, 32)], ("tok", name, 1), to_x[3])

    def forward(c):
        for where, key in chunk_tokens(c):
            arrived(where, key)
        send(T.at[c, core], T.at[c, core], ("fwd", c), to_core)
        if CHUNKS[c] == "z":
            for d in (1, 3, 2):
                name = "zx%d" % (4 - d)
                send(T.at[c, core], T.at[CHUNKS.index(name), core], ("tok", name), to_x[d])

    def gate_up(c):
        if CHUNKS[c] == "own":
            own_copy.wait()
        arrived(T.at[c, other], ("fwd", c))

        def tile(n0, width):
            rows = T[c].reshape(128, K)
            part = jnp.dot(rows, W[:, pl.ds(n0, width)], preferred_element_type=F32)
            PT[c, :, :, pl.ds(n0, width)] = encode(part).reshape(8, 16, width)

        def step(n, carry):
            if c == 0:
                for t in range(3):

                    @pl.when(n == t)
                    def _():
                        for i in W_FOR_TILE[t]:
                            w_copies[i].wait()

            tile(pl.multiple_of(n * 1024, 1024), 1024)
            return carry

        lax.fori_loop(0, 3, step, 0)
        if c == 0:
            w_copies[4].wait()
        tile(3072, 256)
        send(PT.at[c, own(y2, 0)], RL.at[c, 0], ("far+", c), to_yp)
        send(PT.at[c, own(y2, 1)], RL.at[c, 1], ("far-", c), to_ym)
        send(PT.at[c, own(yp, 1)], RM.at[c, 1], ("near+", c), to_yp)
        send(PT.at[c, own(ym, 0)], RP.at[c, 0], ("near-", c), to_ym)
        if c == 0:
            wd_copy.start()

    def relay(c):
        arrived(RL.at[c, 0], ("far+", c))
        o = own(yp, 0)
        PT[c, o] = recode(decode(PT[c, o]) + decode(RL[c, 0]))
        send(PT.at[c, o], RM.at[c, 0], ("via+", c), to_yp)
        arrived(RL.at[c, 1], ("far-", c))
        o = own(ym, 1)
        PT[c, o] = recode(decode(PT[c, o]) + decode(RL[c, 1]))
        send(PT.at[c, o], RP.at[c, 1], ("via-", c), to_ym)

    def over_y(c):
        arrived(RM.at[c, 1], ("near+", c))
        arrived(RP.at[c, 0], ("near-", c))
        arrived(RM.at[c, 0], ("via+", c))
        arrived(RP.at[c, 1], ("via-", c))
        o = own(y, zo)
        PT[c, o] = recode(decode(PT[c, o]) + decode(RM[c, zo]) + decode(RP[c, zo]))
        send(PT.at[c, o], ZR.at[c], ("z_hi", c), to_zh)

    def hidden(c):
        arrived(ZR.at[c], ("z_hi", c))
        o = own(y, zh)

        def total(cols):
            return (
                decode(PT[c, o, :, cols]) + decode(RM[c, zh, :, cols])
                + decode(RP[c, zh, :, cols]) + decode(ZR[c, :, cols])
            )

        gate = total(pl.ds(0, N)) * (gs[...] * (1.0 / LIFT))[None, :]
        up = total(pl.ds(N, N)) * (us[...] * (1.0 / LIFT))[None, :]
        H[c, o] = (jax.nn.silu(gate) * up).astype(BF)
        rows = H.at[c, o]
        send(rows, rows, ("h+", c), to_yp)
        send(rows, rows, ("h-", c), to_ym)
        send(rows, rows, ("hz", c), to_zh)
        if c in DIRECT:
            send(rows, rows, ("hz+", c), to_zh_yp)
            send(rows, rows, ("hz-", c), to_zh_ym)
            send(rows, rows, ("h2", c), to_y2)
            send(rows, rows, ("hz2", c), to_zh_y2)

    def near(c):
        rows = H.at[c, own(ym, zh)]
        arrived(rows, ("h+", c))
        left = rows.at[:, pl.ds(0, HALF)]
        send(left, left, ("hv+", c), to_yp)
        send(rows, rows, ("hz+", c), to_zh)
        rows = H.at[c, own(yp, zh)]
        arrived(rows, ("h-", c))
        right = rows.at[:, pl.ds(HALF, N - HALF)]
        send(right, right, ("hv-", c), to_ym)
        send(rows, rows, ("hz-", c), to_zh)

    def far(c):
        rows = H.at[c, own(y2, zh)]
        arrived(rows.at[:, pl.ds(0, HALF)], ("hv+", c))
        arrived(rows.at[:, pl.ds(HALF, N - HALF)], ("hv-", c))
        send(rows, rows, ("hz2", c), to_zh)

    def down_tile(c, n):
        cols = pl.ds(n * 1024, 1024) if isinstance(n, int) else pl.ds(pl.multiple_of(n * 1024, 1024), 1024)
        rows = H[c].reshape(128, N)
        part = jnp.dot(rows, WD[:, cols], preferred_element_type=F32)
        D[c % 2, :, :, cols] = part.reshape(2, 64, 1024)

    def before_down(c):
        if c in DIRECT:
            arrived(H.at[c, own(ym, zh)], ("h+", c))
            arrived(H.at[c, own(yp, zh)], ("h-", c))
            arrived(H.at[c, own(y2, zh)], ("h2", c))
        arrived(H.at[c, own(y, zo)], ("hz", c))
        arrived(H.at[c, own(ym, zo)], ("hz+", c))
        arrived(H.at[c, own(yp, zo)], ("hz-", c))
        arrived(H.at[c, own(y2, zo)], ("hz2", c))
        if c == 0:
            wd_copy.wait()
        if c >= 2:
            on_way.pop(("core", c - 2)).wait_send()

    def down(c):
        before_down(c)

        def step(n, carry):
            down_tile(c, n)
            return carry

        lax.fori_loop(0, 2, step, 0)
        send(D.at[c % 2, other], CR.at[c], ("core", c), to_core)

    def down_part(c, n):
        if n == 0:
            before_down(c)
        down_tile(c, n)
        cols = pl.ds(n * 1024, 1024)
        send(D.at[c % 2, other, :, cols], CR.at[c, :, cols], ("core", c, n), to_core)

    def add_cores(c, cols, tag):
        name = CHUNKS[c]
        arrived(CR.at[c, :, cols], ("core", c) + tag)
        total = D[c % 2, core, :, cols] + CR[c, :, cols]
        if name not in ALONG_X:
            ACC[("own", "z").index(name), :, cols] = total
            return
        XS[c, :, cols] = total.astype(BF)
        ways = ALONG_X[name]
        rows = 64 // len(ways)
        for i, d in enumerate(ways):
            part = pl.ds(i * rows, rows)
            send(XS.at[c, part, cols], XR.at[c, part, cols], ("x", c, i) + tag, to_x[d])

    def over_core(c):
        add_cores(c, pl.ds(0, M), ())

    def sums_arrived(c):
        ways = ALONG_X[CHUNKS[c]]
        rows = 64 // len(ways)
        for i in range(len(ways)):
            part = pl.ds(i * rows, rows)
            if c in SPLIT:
                for n in range(2):
                    cols = pl.ds(n * 1024, 1024)
                    arrived(XR.at[c, part, cols], ("x", c, i, n))
            else:
                arrived(XR.at[c, part], ("x", c, i))

    def partner(_):
        total = ACC[1]
        for name in ("zx1", "zx2", "zx3"):
            c = CHUNKS.index(name)
            sums_arrived(c)
            total = total + XR[c].astype(F32)
        ZLB[...] = total.astype(BF)
        send(ZLB, ZLR, ("z_lo",), to_zl)

    own_key, z_key = ("fwd", CHUNKS.index("own")), ("tok", "z")
    send(tok, T.at[CHUNKS.index("own"), core], own_key, to_core)
    send(tok, T.at[CHUNKS.index("z"), core], z_key, to_zl)

    steps = dict(
        send_far=send_far, send_near=send_near, forward=forward, gate_up=gate_up, relay=relay, over_y=over_y,
        hidden=hidden, near=near, far=far, down=down, over_core=over_core, partner=partner,
        down_a=lambda c: down_part(c, 0), down_b=lambda c: down_part(c, 1),
        over_core_a=lambda c: add_cores(c, pl.ds(0, 1024), (0,)),
        over_core_b=lambda c: add_cores(c, pl.ds(1024, 1024), (1,)),
    )
    for name, c in ORDER:
        steps[name](c)

    c2, ca, cb = CHUNKS.index("x2"), CHUNKS.index("mixA"), CHUNKS.index("mixB")
    sums_arrived(c2)
    base = ACC[0] + XR[c2].astype(F32)
    arrived(ZLR, ("z_lo",))
    base = base + ZLR[...].astype(F32)
    for i, c in enumerate((ca, cb)):
        sums_arrived(c)
        rows = slice(32 * i, 32 * i + 32)
        total = base[rows] + XR[c, 0:32].astype(F32) + XR[c, 32:64].astype(F32)
        out[rows, :] = (total * ds[...][None, :]).astype(BF)

    for c in on_way.values():
        c.wait_send()


def on_device(tokens, gate_weight, up_weight, gate_scale, up_scale, down_weight, down_scale):
    hbm, vmem = pl.BlockSpec(memory_space=pl.ANY), pl.BlockSpec(memory_space=pltpu.VMEM)
    return pl.pallas_call(
        body,
        name="gated_layer",
        out_shape=jax.ShapeDtypeStruct((64, M), BF),
        in_specs=[hbm, hbm, hbm, vmem, vmem, hbm, vmem],
        out_specs=vmem,
        scratch_shapes=[
            pltpu.VMEM((K, N2), BF),
            pltpu.VMEM((N, M), BF),
            pltpu.VMEM((NC, 2, 64, K), BF),
            pltpu.VMEM((NC, 8, 16, N2), BF),
            pltpu.VMEM((NC, 2, 16, N2), BF),
            pltpu.VMEM((NC, 2, 16, N2), BF),
            pltpu.VMEM((NC, 2, 16, N2), BF),
            pltpu.VMEM((NC, 16, N2), BF),
            pltpu.VMEM((NC, 8, 16, N), BF),
            pltpu.VMEM((2, 2, 64, M), F32),
            pltpu.VMEM((NC, 64, M), F32),
            pltpu.VMEM((NC, 64, M), BF),
            pltpu.VMEM((NC, 64, M), BF),
            pltpu.VMEM((2, 64, M), F32),
            pltpu.VMEM((64, M), BF),
            pltpu.VMEM((64, M), BF),
            pltpu.SemaphoreType.DMA((NSEM,)),
            pltpu.SemaphoreType.DMA((NSEM,)),
            pltpu.SemaphoreType.DMA((7,)),
        ],
        compiler_params=pltpu.CompilerParams(
            collective_id=0, has_side_effects=True, vmem_limit_bytes=62 * 2**20
        ),
        cost_estimate=pl.CostEstimate(
            flops=2 * 1024 * K * N2 + 2 * 1024 * N * M, bytes_accessed=2 * (K * N2 + N * M), transcendentals=0
        ),
    )(tokens, gate_weight, up_weight, gate_scale, up_scale, down_weight, down_scale)


def solution(mesh):
    return jax.shard_map(
        on_device,
        mesh=mesh,
        in_specs=(
            P("gy", "gx"),
            P("gx", "gy"),
            P("gx", "gy"),
            P("gy"),
            P("gy"),
            P("gy", "gx"),
            P("gx"),
        ),
        out_specs=P("gy", "gx"),
        check_vma=False,
    )
```

```python
import jax
import jax.numpy as jnp
from jax import lax
from jax.experimental import pallas as pl
from jax.experimental.pallas import tpu as pltpu
from jax.sharding import PartitionSpec as P

MESH = pl.DeviceIdType.MESH
BF, F32 = jnp.bfloat16, jnp.float32
NC = 8
K, N, N2, M = 2048, 1664, 3328, 2048
HALF = 896
LIFT = 2.0**50
TINY = 1e-37

CHUNKS = ("own", "x2", "z", "zx2", "zx1", "zx3", "mixA", "mixB")
DIRECT = (6, 7)
SPLIT = (6, 7)
RS_GROUPS = (0, 6, 7)
ORDER = (
    ("send_far", 0), ("gate_up", 0), ("relay_a", 0), ("forward", 1), ("forward", 2), ("relay_b", 0), ("near_sums", 0),
    ("gate_up", 1), ("near_sums", 1), ("gate_up", 2), ("forward", 4), ("relay", 1), ("over_y", 0), ("near_sums", 2),
    ("hidden", 0), ("forward", 3), ("relay", 2), ("gate_up", 3), ("near_sums", 3), ("over_y", 1), ("near", 0),
    ("over_y", 2), ("send_near", 0), ("relay", 3), ("gate_up", 4), ("far", 0), ("near_sums", 4), ("hidden", 2),
    ("forward", 5), ("over_y", 3), ("relay", 4), ("hidden", 1), ("forward", 6), ("gate_up", 5), ("near", 2),
    ("over_y", 4), ("near", 1), ("near_sums", 5), ("down", 0), ("relay", 5), ("far", 1), ("hidden", 3), ("far", 2),
    ("gate_up", 6), ("hidden", 4), ("over_y", 5), ("near", 3), ("forward", 7), ("over_core", 0), ("relay_a", 6),
    ("down", 1), ("near", 4), ("far", 3), ("near_sums", 6), ("hidden", 5), ("gate_up", 7), ("over_core", 1),
    ("far", 4), ("over_y_a", 6), ("down", 2), ("near", 5), ("relay_b", 6), ("down", 3), ("relay_a", 7), ("far", 5),
    ("near_sums", 7), ("over_y_b", 6), ("over_core", 2), ("relay_b", 7), ("over_core", 3), ("hidden_a", 6),
    ("down", 4), ("over_y_a", 7), ("down", 5), ("over_y_b", 7), ("hidden_b", 6), ("over_core", 4), ("over_core", 5),
    ("hidden_a", 7), ("down_first", 6), ("hidden_b", 7), ("down_a", 6), ("down_b", 6), ("over_core_a", 6),
    ("down_first", 7), ("partner", 0), ("down_a", 7), ("over_core_b", 6), ("down_b", 7), ("over_core_a", 7),
    ("over_core_b", 7),
)

ALONG_X = {"x2": (2,), "zx1": (1,), "zx2": (2,), "zx3": (3,), "mixA": (1, 3), "mixB": (1, 3)}
PIECES = ((0, 0, 896, 0), (1, 0, 896, 896), (0, 896, 768, 1792), (1, 896, 768, 2560))
W_FOR_TILE = ((0, 1), (2,), (3,), ())
GROUPS = ((0, 0, 896), (1792, 896, 768))
NSEM = 208


def sum_columns(g):
    return pl.ds(0, N2) if g is None else pl.ds(GROUPS[g][0], 2 * GROUPS[g][2])


def hidden_columns(g):
    return pl.ds(0, N) if g is None else pl.ds(GROUPS[g][1], GROUPS[g][2])


def parts(c, chunks):
    return (0, 1) if c in chunks else (None,)


def encode(v):
    v = v * LIFT
    return (v * jnp.abs(v)).astype(BF)


def decode(q):
    q = q.astype(F32)
    return q * lax.rsqrt(jnp.maximum(jnp.abs(q), TINY))


def recode(s):
    return (s * jnp.abs(s)).astype(BF)


def body(tok, wg, wu, gs_in, us_in, wd, ds_in, out, gs, us, ds, W, WD, T, PT, RL, RM, RP, ZR, H, D, CR, XS, XR, ACC, ZLB, ZLR, ssem, rsem, lsem):
    gx, gy = lax.axis_index("gx"), lax.axis_index("gy")
    zh, y = gx // 4, lax.rem(gx, 4)
    zl, x, core = gy // 8, lax.rem(gy // 2, 4), lax.rem(gy, 2)
    zo, other = 1 - zh, 1 - core
    yp, ym, y2 = lax.rem(y + 1, 4), lax.rem(y + 3, 4), lax.rem(y + 2, 4)

    def at(zh_=zh, y_=y, zl_=zl, x_=x, core_=core):
        return (zh_ * 4 + y_, zl_ * 8 + x_ * 2 + core_)

    to_yp, to_ym, to_y2 = at(y_=yp), at(y_=ym), at(y_=y2)
    to_zh, to_zh_yp, to_zh_ym, to_zh_y2 = at(zh_=zo), at(zh_=zo, y_=yp), at(zh_=zo, y_=ym), at(zh_=zo, y_=y2)
    to_zl, to_core = at(zl_=1 - zl), at(core_=other)
    to_x = [None] + [at(x_=lax.rem(x + d, 4)) for d in (1, 2, 3)]

    def own(y_, z_):
        return y_ * 2 + z_

    semaphore, on_way = {}, {}

    def copy(src, dst, key, to):
        k = semaphore.setdefault(key, len(semaphore))
        return pltpu.make_async_remote_copy(
            src_ref=src, dst_ref=dst, send_sem=ssem.at[k], recv_sem=rsem.at[k], device_id=to, device_id_type=MESH
        )

    def send(src, dst, key, to):
        on_way[key] = copy(src, dst, key, to)
        on_way[key].start()

    def arrived(dst, key):
        copy(dst, dst, key, to_core).wait_recv()

    w_copies = [
        pltpu.make_async_copy((wg, wu)[m].at[:, pl.ds(c0, n)], W.at[:, pl.ds(d0, n)], lsem.at[i])
        for i, (m, c0, n, d0) in enumerate(PIECES)
    ]
    own_copy = pltpu.make_async_copy(tok, T.at[CHUNKS.index("own"), core], lsem.at[5])
    wd_copy = pltpu.make_async_copy(wd, WD, lsem.at[6])
    scale_copies = [
        pltpu.make_async_copy(a, b, lsem.at[7 + i]) for i, (a, b) in enumerate(((gs_in, gs), (us_in, us), (ds_in, ds)))
    ]
    own_copy.start()
    for c in w_copies + scale_copies:
        c.start()

    barrier = pltpu.get_barrier_semaphore()
    partners = [to_yp, to_ym, to_y2, to_zh, to_zh_yp, to_zh_ym, to_zh_y2, to_zl, to_core] + to_x[1:]
    for p in partners:
        pl.semaphore_signal(barrier, inc=1, device_id=p, device_id_type=MESH)
    pl.semaphore_wait(barrier, len(partners))

    def chunk_tokens(c):
        name = CHUNKS[c]
        if name[:3] == "mix":
            return [(T.at[c, core, pl.ds(32 * i, 32)], ("tok", name, d)) for i, d in enumerate((1, 3))]
        return [(T.at[c, core], ("tok", name))]

    def send_far(_):
        send(tok, T.at[CHUNKS.index("x2"), core], ("tok", "x2"), to_x[2])

    def send_near(_):
        for i, name in enumerate(("mixA", "mixB")):
            c = CHUNKS.index(name)
            rows = tok.at[pl.ds(32 * i, 32)]
            send(rows, T.at[c, core, pl.ds(32, 32)], ("tok", name, 3), to_x[1])
            send(rows, T.at[c, core, pl.ds(0, 32)], ("tok", name, 1), to_x[3])

    def forward(c):
        for where, key in chunk_tokens(c):
            arrived(where, key)
        send(T.at[c, core], T.at[c, core], ("fwd", c), to_core)
        if CHUNKS[c] == "z":
            for d in (1, 3, 2):
                name = "zx%d" % (4 - d)
                send(T.at[c, core], T.at[CHUNKS.index(name), core], ("tok", name), to_x[d])

    def gate_up(c):
        if CHUNKS[c] == "own":
            own_copy.wait()
        arrived(T.at[c, other], ("fwd", c))

        def tile(n0, width):
            rows = T[c].reshape(128, K)
            part = jnp.dot(rows, W[:, pl.ds(n0, width)], preferred_element_type=F32)
            PT[c, :, :, pl.ds(n0, width)] = encode(part).reshape(8, 16, width)

        def far_sums(g):
            cols = sum_columns(g)
            send(PT.at[c, own(y2, 0), :, cols], RL.at[c, 0, :, cols], ("far+", c, g), to_yp)
            send(PT.at[c, own(y2, 1), :, cols], RL.at[c, 1, :, cols], ("far-", c, g), to_ym)

        if c == 0:
            for t in range(2):
                for i in W_FOR_TILE[t]:
                    w_copies[i].wait()
                tile(1024 * t, 1024)
            if c in RS_GROUPS:
                far_sums(0)
            w_copies[3].wait()
            tile(2048, 1024)
        else:

            def step(n, carry):
                tile(pl.multiple_of(n * 1024, 1024), 1024)
                return carry

            lax.fori_loop(0, 3, step, 0)
        tile(3072, 256)
        for g in parts(c, RS_GROUPS):
            if c or g != 0:
                far_sums(g)
        if c == 0:
            wd_copy.start()

    def near_sums(c):
        if c == 0:
            for scale in scale_copies:
                scale.wait()
        for g in parts(c, RS_GROUPS):
            cols = sum_columns(g)
            send(PT.at[c, own(yp, 1), :, cols], RM.at[c, 1, :, cols], ("near+", c, g), to_yp)
            send(PT.at[c, own(ym, 0), :, cols], RP.at[c, 0, :, cols], ("near-", c, g), to_ym)

    def relay(c, g=None):
        cols = sum_columns(g)
        for i, (o, dst, far, via, to) in enumerate(
            ((own(yp, 0), RM, "far+", "via+", to_yp), (own(ym, 1), RP, "far-", "via-", to_ym))
        ):
            arrived(RL.at[c, i, :, cols], (far, c, g))
            PT[c, o, :, cols] = recode(decode(PT[c, o, :, cols]) + decode(RL[c, i, :, cols]))
            send(PT.at[c, o, :, cols], dst.at[c, i, :, cols], (via, c, g), to)

    def over_y(c, g=None):
        for h in parts(c, RS_GROUPS):
            if g is None or g == h:
                cols = sum_columns(h)
                arrived(RM.at[c, 1, :, cols], ("near+", c, h))
                arrived(RP.at[c, 0, :, cols], ("near-", c, h))
                arrived(RM.at[c, 0, :, cols], ("via+", c, h))
                arrived(RP.at[c, 1, :, cols], ("via-", c, h))
        o, cols = own(y, zo), sum_columns(g)
        PT[c, o, :, cols] = recode(
            decode(PT[c, o, :, cols]) + decode(RM[c, zo, :, cols]) + decode(RP[c, zo, :, cols])
        )
        send(PT.at[c, o, :, cols], ZR.at[c, :, cols], ("z_hi", c, g), to_zh)

    def hidden(c, g=None):
        arrived(ZR.at[c, :, sum_columns(g)], ("z_hi", c, g))
        o = own(y, zh)

        def total(cols):
            return (
                decode(PT[c, o, :, cols]) + decode(RM[c, zh, :, cols])
                + decode(RP[c, zh, :, cols]) + decode(ZR[c, :, cols])
            )

        for h in (0, 1):
            if g is None or g == h:
                first, _, width = GROUPS[h]
                units = hidden_columns(h)
                gate = total(pl.ds(first, width)) * (gs[units] * (1.0 / LIFT))[None, :]
                up = total(pl.ds(first + width, width)) * (us[units] * (1.0 / LIFT))[None, :]
                H[c, o, :, units] = (jax.nn.silu(gate) * up).astype(BF)
        rows = H.at[c, o, :, hidden_columns(g)]
        send(rows, rows, ("h+", c, g), to_yp)
        send(rows, rows, ("h-", c, g), to_ym)
        send(rows, rows, ("hz", c, g), to_zh)
        if c in DIRECT:
            send(rows, rows, ("hz+", c, g), to_zh_yp)
            send(rows, rows, ("hz-", c, g), to_zh_ym)
            send(rows, rows, ("h2", c, g), to_y2)
            send(rows, rows, ("hz2", c, g), to_zh_y2)

    def near(c):
        rows = H.at[c, own(ym, zh)]
        arrived(rows, ("h+", c, None))
        left = rows.at[:, pl.ds(0, HALF)]
        send(left, left, ("hv+", c), to_yp)
        send(rows, rows, ("hz+", c, None), to_zh)
        rows = H.at[c, own(yp, zh)]
        arrived(rows, ("h-", c, None))
        right = rows.at[:, pl.ds(HALF, N - HALF)]
        send(right, right, ("hv-", c), to_ym)
        send(rows, rows, ("hz-", c, None), to_zh)

    def far(c):
        rows = H.at[c, own(y2, zh)]
        arrived(rows.at[:, pl.ds(0, HALF)], ("hv+", c))
        arrived(rows.at[:, pl.ds(HALF, N - HALF)], ("hv-", c))
        send(rows, rows, ("hz2", c, None), to_zh)

    def down_tile(c, n):
        cols = pl.ds(pl.multiple_of(n * 1024, 1024), 1024)
        rows = H[c].reshape(128, N)
        part = jnp.dot(rows, WD[:, cols], preferred_element_type=F32)
        D[c % 2, :, :, cols] = part.reshape(2, 64, 1024)

    def hidden_arrived(c, g):
        keys = [("hz", y, zo), ("hz+", ym, zo), ("hz-", yp, zo), ("hz2", y2, zo)]
        if c in DIRECT:
            keys += [("h+", ym, zh), ("h-", yp, zh), ("h2", y2, zh)]
        for key, y_, z_ in keys:
            arrived(H.at[c, own(y_, z_), :, hidden_columns(g)], (key, c, g))

    def before_down(c):
        if c == 0:
            wd_copy.wait()
        if c >= 2:
            on_way.pop(("core", c - 2)).wait_send()

    def down(c):
        hidden_arrived(c, None)
        before_down(c)

        def step(n, carry):
            down_tile(c, n)
            return carry

        lax.fori_loop(0, 2, step, 0)
        send(D.at[c % 2, other], CR.at[c], ("core", c), to_core)

    def down_first(c):
        hidden_arrived(c, 0)
        before_down(c)

        def step(n, carry):
            cols = pl.ds(pl.multiple_of(n * 1024, 1024), 1024)
            rows = H[c, :, :, pl.ds(0, 896)].reshape(128, 896)
            part = jnp.dot(rows, WD[pl.ds(0, 896), cols], preferred_element_type=F32)
            D[c % 2, :, :, cols] = part.reshape(2, 64, 1024)
            return carry

        lax.fori_loop(0, 2, step, 0)

    def down_rest(c, n):
        if n == 0:
            hidden_arrived(c, 1)
        cols = pl.ds(n * 1024, 1024)
        rows = H[c, :, :, pl.ds(896, 768)].reshape(128, 768)
        part = jnp.dot(rows, WD[pl.ds(896, 768), cols], preferred_element_type=F32)
        D[c % 2, :, :, cols] += part.reshape(2, 64, 1024)
        send(D.at[c % 2, other, :, cols], CR.at[c, :, cols], ("core", c, n), to_core)

    def add_cores(c, cols, tag):
        name = CHUNKS[c]
        arrived(CR.at[c, :, cols], ("core", c) + tag)
        total = D[c % 2, core, :, cols] + CR[c, :, cols]
        if name not in ALONG_X:
            ACC[("own", "z").index(name), :, cols] = total
            return
        XS[c, :, cols] = total.astype(BF)
        ways = ALONG_X[name]
        rows = 64 // len(ways)
        for i, d in enumerate(ways):
            part = pl.ds(i * rows, rows)
            send(XS.at[c, part, cols], XR.at[c, part, cols], ("x", c, i) + tag, to_x[d])

    def over_core(c):
        add_cores(c, pl.ds(0, M), ())

    def sums_arrived(c):
        ways = ALONG_X[CHUNKS[c]]
        rows = 64 // len(ways)
        for i in range(len(ways)):
            part = pl.ds(i * rows, rows)
            if c in SPLIT:
                for n in range(2):
                    cols = pl.ds(n * 1024, 1024)
                    arrived(XR.at[c, part, cols], ("x", c, i, n))
            else:
                arrived(XR.at[c, part], ("x", c, i))

    def partner(_):
        total = ACC[1]
        for name in ("zx1", "zx2", "zx3"):
            c = CHUNKS.index(name)
            sums_arrived(c)
            total = total + XR[c].astype(F32)
        ZLB[...] = total.astype(BF)
        send(ZLB, ZLR, ("z_lo",), to_zl)

    own_key, z_key = ("fwd", CHUNKS.index("own")), ("tok", "z")
    send(tok, T.at[CHUNKS.index("own"), core], own_key, to_core)
    send(tok, T.at[CHUNKS.index("z"), core], z_key, to_zl)

    steps = dict(
        send_far=send_far, send_near=send_near, forward=forward, gate_up=gate_up, near_sums=near_sums, relay=relay, over_y=over_y,
        hidden=hidden, near=near, far=far, down=down, over_core=over_core, partner=partner,
        relay_a=lambda c: relay(c, 0), relay_b=lambda c: relay(c, 1),
        over_y_a=lambda c: over_y(c, 0), over_y_b=lambda c: over_y(c, 1),
        hidden_a=lambda c: hidden(c, 0), hidden_b=lambda c: hidden(c, 1),
        down_first=down_first, down_a=lambda c: down_rest(c, 0), down_b=lambda c: down_rest(c, 1),
        over_core_a=lambda c: add_cores(c, pl.ds(0, 1024), (0,)),
        over_core_b=lambda c: add_cores(c, pl.ds(1024, 1024), (1,)),
    )
    for name, c in ORDER:
        steps[name](c)

    for key in list(on_way):
        if key[0] not in ("x", "z_lo", "core") or (key[0] == "x" and key[1] not in SPLIT):
            on_way.pop(key).wait_send()

    c2, ca, cb = CHUNKS.index("x2"), CHUNKS.index("mixA"), CHUNKS.index("mixB")
    sums_arrived(c2)
    base = ACC[0] + XR[c2].astype(F32)
    arrived(ZLR, ("z_lo",))
    base = base + ZLR[...].astype(F32)
    for i, c in enumerate((ca, cb)):
        sums_arrived(c)
        rows = slice(32 * i, 32 * i + 32)
        total = base[rows] + XR[c, 0:32].astype(F32) + XR[c, 32:64].astype(F32)
        out[rows, :] = (total * ds[...][None, :]).astype(BF)

    for c in on_way.values():
        c.wait_send()


def on_device(tokens, gate_weight, up_weight, gate_scale, up_scale, down_weight, down_scale):
    hbm, vmem = pl.BlockSpec(memory_space=pl.ANY), pl.BlockSpec(memory_space=pltpu.VMEM)
    return pl.pallas_call(
        body,
        name="gated_layer",
        out_shape=jax.ShapeDtypeStruct((64, M), BF),
        in_specs=[hbm] * 7,
        out_specs=vmem,
        scratch_shapes=[
            pltpu.VMEM((N,), F32),
            pltpu.VMEM((N,), F32),
            pltpu.VMEM((M,), F32),
            pltpu.VMEM((K, N2), BF),
            pltpu.VMEM((N, M), BF),
            pltpu.VMEM((NC, 2, 64, K), BF),
            pltpu.VMEM((NC, 8, 16, N2), BF),
            pltpu.VMEM((NC, 2, 16, N2), BF),
            pltpu.VMEM((NC, 2, 16, N2), BF),
            pltpu.VMEM((NC, 2, 16, N2), BF),
            pltpu.VMEM((NC, 16, N2), BF),
            pltpu.VMEM((NC, 8, 16, N), BF),
            pltpu.VMEM((2, 2, 64, M), F32),
            pltpu.VMEM((NC, 64, M), F32),
            pltpu.VMEM((NC, 64, M), BF),
            pltpu.VMEM((NC, 64, M), BF),
            pltpu.VMEM((2, 64, M), F32),
            pltpu.VMEM((64, M), BF),
            pltpu.VMEM((64, M), BF),
            pltpu.SemaphoreType.DMA((NSEM,)),
            pltpu.SemaphoreType.DMA((NSEM,)),
            pltpu.SemaphoreType.DMA((10,)),
        ],
        compiler_params=pltpu.CompilerParams(
            collective_id=0, has_side_effects=True, vmem_limit_bytes=62 * 2**20
        ),
        cost_estimate=pl.CostEstimate(
            flops=2 * 1024 * K * N2 + 2 * 1024 * N * M, bytes_accessed=2 * (K * N2 + N * M), transcendentals=0
        ),
    )(tokens, gate_weight, up_weight, gate_scale, up_scale, down_weight, down_scale)


def solution(mesh):
    return jax.shard_map(
        on_device,
        mesh=mesh,
        in_specs=(
            P("gy", "gx"),
            P("gx", "gy"),
            P("gx", "gy"),
            P("gy"),
            P("gy"),
            P("gy", "gx"),
            P("gx"),
        ),
        out_specs=P("gy", "gx"),
        check_vma=False,
    )
```

```python
import jax
import jax.numpy as jnp
from jax import lax
from jax.experimental import pallas as pl
from jax.experimental.pallas import tpu as pltpu
from jax.sharding import PartitionSpec as P

MESH = pl.DeviceIdType.MESH
BF, F32 = jnp.bfloat16, jnp.float32
NC = 8
K, N, N2, M = 2048, 1664, 3328, 2048
HALF = 896
LIFT = 2.0**50
TINY = 1e-37

CHUNKS = ("own", "z", "x2", "zx2", "zmixA", "zmixB", "mixA", "mixB")
DIRECT = (7,)
Z_SUMS_FIRST = (3,)
Z_FIRST = (6,)
SPLIT = (6, 7)
RS_GROUPS = (0, 6, 7)
ORDER = (
    ("send_far", 0), ("gate_up", 0), ("near_sums", 0), ("forward", 1), ("relay_a", 0), ("relay_b", 0), ("forward", 2),
    ("gate_up", 1), ("near_sums", 1), ("over_y", 0), ("gate_up", 2), ("forward", 3), ("hidden", 0), ("near_sums", 2),
    ("gate_up", 3), ("send_near", 0), ("relay", 1), ("forward", 4), ("forward", 5), ("relay", 2), ("gate_up", 4),
    ("gate_up", 5), ("near_sums", 4), ("over_y", 1), ("over_y", 2), ("near", 0), ("relay", 4), ("near_sums", 3),
    ("forward", 6), ("far", 0), ("hidden", 2), ("over_y", 4), ("forward", 7), ("hidden", 1), ("relay", 3),
    ("near_sums", 5), ("down", 0), ("near", 2), ("near", 1), ("relay", 5), ("hidden", 3), ("gate_up", 6),
    ("over_core", 0), ("far", 1), ("far", 2), ("hidden", 4), ("over_y", 5), ("near", 3), ("relay_a", 6), ("down", 1),
    ("relay_b", 6), ("near", 4), ("near_sums", 6), ("gate_up", 7), ("far", 3), ("down", 2), ("over_core", 1),
    ("far", 4), ("over_y_a", 6), ("hidden", 5), ("near_sums", 7), ("over_y_b", 6), ("relay_a", 7), ("over_core", 2),
    ("down", 3), ("near", 5), ("down", 4), ("hidden_a", 6), ("relay_b", 7), ("hidden_b", 6), ("over_core", 3),
    ("over_y_a", 7), ("far", 5), ("pass_on_a", 6), ("over_core", 4), ("over_y_b", 7), ("pass_on_b", 6),
    ("hidden_a", 7), ("down", 5), ("hidden_b", 7), ("down_first", 6), ("down_a", 6), ("down_b", 6), ("over_core", 5),
    ("partner_a", 0), ("over_core_a", 6), ("down_first", 7), ("down_a", 7), ("down_b", 7), ("over_core_b", 6),
    ("over_core_a", 7), ("partner_b", 0), ("over_core_b", 7),
)

ALONG_X = {"x2": (2,), "zx1": (1,), "zx2": (2,), "zx3": (3,), "mixA": (1, 3), "mixB": (1, 3), "zmixA": (1, 3), "zmixB": (1, 3)}
PIECES = ((0, 0, 896, 0), (1, 0, 896, 896), (0, 896, 768, 1792), (1, 896, 768, 2560))
W_FOR_TILE = ((0, 1), (2,), (3,), ())
GROUPS = ((0, 0, 896), (1792, 896, 768))
NSEM = 208


def sum_columns(g):
    return pl.ds(0, N2) if g is None else pl.ds(GROUPS[g][0], 2 * GROUPS[g][2])


def hidden_columns(g):
    return pl.ds(0, N) if g is None else pl.ds(GROUPS[g][1], GROUPS[g][2])


def parts(c, chunks):
    return (0, 1) if c in chunks else (None,)


def encode(v):
    v = v * LIFT
    return (v * jnp.abs(v)).astype(BF)


def decode(q):
    q = q.astype(F32)
    return q * lax.rsqrt(jnp.maximum(jnp.abs(q), TINY))


def recode(s):
    return (s * jnp.abs(s)).astype(BF)


def body(tok, wg, wu, gs_in, us_in, wd, ds_in, out, gs, us, ds, W, WD, T, PT, RL, RM, RP, ZX, ZR, H, D, CR, XS, XR, ACC, ZLB, ZLR, ssem, rsem, lsem):
    gx, gy = lax.axis_index("gx"), lax.axis_index("gy")
    zh, y = gx // 4, lax.rem(gx, 4)
    zl, x, core = gy // 8, lax.rem(gy // 2, 4), lax.rem(gy, 2)
    zo, other = 1 - zh, 1 - core
    yp, ym, y2 = lax.rem(y + 1, 4), lax.rem(y + 3, 4), lax.rem(y + 2, 4)

    def at(zh_=zh, y_=y, zl_=zl, x_=x, core_=core):
        return (zh_ * 4 + y_, zl_ * 8 + x_ * 2 + core_)

    to_yp, to_ym, to_y2 = at(y_=yp), at(y_=ym), at(y_=y2)
    to_zh, to_zh_yp, to_zh_ym, to_zh_y2 = at(zh_=zo), at(zh_=zo, y_=yp), at(zh_=zo, y_=ym), at(zh_=zo, y_=y2)
    to_zl, to_core = at(zl_=1 - zl), at(core_=other)
    to_x = [None] + [at(x_=lax.rem(x + d, 4)) for d in (1, 2, 3)]

    def own(y_, z_):
        return y_ * 2 + z_

    semaphore, on_way = {}, {}

    def copy(src, dst, key, to):
        k = semaphore.setdefault(key, len(semaphore))
        return pltpu.make_async_remote_copy(
            src_ref=src, dst_ref=dst, send_sem=ssem.at[k], recv_sem=rsem.at[k], device_id=to, device_id_type=MESH
        )

    def send(src, dst, key, to):
        on_way[key] = copy(src, dst, key, to)
        on_way[key].start()

    def arrived(dst, key):
        copy(dst, dst, key, to_core).wait_recv()

    w_copies = [
        pltpu.make_async_copy((wg, wu)[m].at[:, pl.ds(c0, n)], W.at[:, pl.ds(d0, n)], lsem.at[i])
        for i, (m, c0, n, d0) in enumerate(PIECES)
    ]
    own_copy = pltpu.make_async_copy(tok, T.at[CHUNKS.index("own"), core], lsem.at[5])
    wd_copy = pltpu.make_async_copy(wd, WD, lsem.at[6])
    scale_copies = [
        pltpu.make_async_copy(a, b, lsem.at[7 + i]) for i, (a, b) in enumerate(((gs_in, gs), (us_in, us), (ds_in, ds)))
    ]
    own_copy.start()
    for c in w_copies + scale_copies:
        c.start()

    barrier = pltpu.get_barrier_semaphore()
    partners = [to_yp, to_ym, to_y2, to_zh, to_zh_yp, to_zh_ym, to_zh_y2, to_zl, to_core] + to_x[1:]
    for p in partners:
        pl.semaphore_signal(barrier, inc=1, device_id=p, device_id_type=MESH)
    pl.semaphore_wait(barrier, len(partners))

    def chunk_tokens(c):
        name = CHUNKS[c]
        if "mix" in name:
            return [(T.at[c, core, pl.ds(32 * i, 32)], ("tok", name, d)) for i, d in enumerate((1, 3))]
        return [(T.at[c, core], ("tok", name))]

    def send_far(_):
        send(tok, T.at[CHUNKS.index("x2"), core], ("tok", "x2"), to_x[2])

    def mixed(rows, name):
        c = CHUNKS.index(name)
        rows = rows.at[pl.ds(32 * "AB".index(name[-1]), 32)]
        send(rows, T.at[c, core, pl.ds(32, 32)], ("tok", name, 3), to_x[1])
        send(rows, T.at[c, core, pl.ds(0, 32)], ("tok", name, 1), to_x[3])

    def send_near(_):
        mixed(tok, "mixA")
        mixed(tok, "mixB")

    def forward(c):
        for where, key in chunk_tokens(c):
            arrived(where, key)
        send(T.at[c, core], T.at[c, core], ("fwd", c), to_core)
        if CHUNKS[c] == "z":
            for name in CHUNKS:
                if name[:2] == "zx":
                    send(T.at[c, core], T.at[CHUNKS.index(name), core], ("tok", name), to_x[4 - int(name[2])])
                if name[:4] == "zmix":
                    mixed(T.at[c, core], name)

    def gate_up(c):
        if CHUNKS[c] == "own":
            own_copy.wait()
        arrived(T.at[c, other], ("fwd", c))

        def tile(n0, width):
            rows = T[c].reshape(128, K)
            part = jnp.dot(rows, W[:, pl.ds(n0, width)], preferred_element_type=F32)
            PT[c, :, :, pl.ds(n0, width)] = encode(part).reshape(8, 16, width)

        def far_sums(g):
            cols = sum_columns(g)
            send(PT.at[c, own(y2, 0), :, cols], RL.at[c, 0, :, cols], ("far+", c, g), to_yp)
            send(PT.at[c, own(y2, 1), :, cols], RL.at[c, 1, :, cols], ("far-", c, g), to_ym)

        if c == 0:
            for t in range(2):
                for i in W_FOR_TILE[t]:
                    w_copies[i].wait()
                tile(1024 * t, 1024)
            if c in RS_GROUPS:
                far_sums(0)
            w_copies[3].wait()
            tile(2048, 1024)
        else:

            def step(n, carry):
                tile(pl.multiple_of(n * 1024, 1024), 1024)
                return carry

            lax.fori_loop(0, 3, step, 0)
        tile(3072, 256)
        if c in Z_SUMS_FIRST:
            for j in range(4):
                send(PT.at[c, own(j, zo)], ZX.at[j], ("z_first", c, j), to_zh)
        else:
            for g in parts(c, RS_GROUPS):
                if c or g != 0:
                    far_sums(g)
        if c == 0:
            wd_copy.start()

    def z_sums(c):
        for j in range(4):
            arrived(ZX.at[j], ("z_first", c, j))
        a, b = sum_columns(0), sum_columns(1)

        def add(y_):
            o = own(y_, zh)
            PT[c, o] = recode(decode(PT[c, o]) + decode(ZX[y_]))
            return PT.at[c, o]

        far = add(y2)
        send(far.at[:, a], RL.at[c, 0, :, a], ("far+", c), to_yp)
        send(far.at[:, b], RL.at[c, 1, :, b], ("far-", c), to_ym)
        send(add(yp).at[:, b], RM.at[c, 0, :, b], ("near+", c), to_yp)
        send(add(ym).at[:, a], RP.at[c, 0, :, a], ("near-", c), to_ym)
        add(y)

    def relay_z_sums(c):
        for i, (y_, g, dst, far, via, to) in enumerate(
            ((yp, 0, RM, "far+", "via+", to_yp), (ym, 1, RP, "far-", "via-", to_ym))
        ):
            o, cols = own(y_, zh), sum_columns(g)
            arrived(RL.at[c, i, :, cols], (far, c))
            PT[c, o, :, cols] = recode(decode(PT[c, o, :, cols]) + decode(RL[c, i, :, cols]))
            send(PT.at[c, o, :, cols], dst.at[c, 0, :, cols], (via, c), to)

    def near_sums(c):
        if c in Z_SUMS_FIRST:
            z_sums(c)
            return
        if c == 0:
            for scale in scale_copies:
                scale.wait()
        for g in parts(c, RS_GROUPS):
            cols = sum_columns(g)
            send(PT.at[c, own(yp, 1), :, cols], RM.at[c, 1, :, cols], ("near+", c, g), to_yp)
            send(PT.at[c, own(ym, 0), :, cols], RP.at[c, 0, :, cols], ("near-", c, g), to_ym)

    def relay(c, g=None):
        if c in Z_SUMS_FIRST:
            relay_z_sums(c)
            return
        cols = sum_columns(g)
        for i, (o, dst, far, via, to) in enumerate(
            ((own(yp, 0), RM, "far+", "via+", to_yp), (own(ym, 1), RP, "far-", "via-", to_ym))
        ):
            arrived(RL.at[c, i, :, cols], (far, c, g))
            PT[c, o, :, cols] = recode(decode(PT[c, o, :, cols]) + decode(RL[c, i, :, cols]))
            send(PT.at[c, o, :, cols], dst.at[c, i, :, cols], (via, c, g), to)

    def over_y(c, g=None):
        for h in parts(c, RS_GROUPS):
            if g is None or g == h:
                cols = sum_columns(h)
                arrived(RM.at[c, 1, :, cols], ("near+", c, h))
                arrived(RP.at[c, 0, :, cols], ("near-", c, h))
                arrived(RM.at[c, 0, :, cols], ("via+", c, h))
                arrived(RP.at[c, 1, :, cols], ("via-", c, h))
        o, cols = own(y, zo), sum_columns(g)
        PT[c, o, :, cols] = recode(
            decode(PT[c, o, :, cols]) + decode(RM[c, zo, :, cols]) + decode(RP[c, zo, :, cols])
        )
        send(PT.at[c, o, :, cols], ZR.at[c, :, cols], ("z_hi", c, g), to_zh)

    def hidden(c, g=None):
        o = own(y, zh)
        if c in Z_SUMS_FIRST:
            for h, plus, minus in ((0, "via+", "near-"), (1, "near+", "via-")):
                arrived(RM.at[c, 0, :, sum_columns(h)], (plus, c))
                arrived(RP.at[c, 0, :, sum_columns(h)], (minus, c))
        else:
            arrived(ZR.at[c, :, sum_columns(g)], ("z_hi", c, g))

        def total(cols):
            if c in Z_SUMS_FIRST:
                return decode(PT[c, o, :, cols]) + decode(RM[c, 0, :, cols]) + decode(RP[c, 0, :, cols])
            return (
                decode(PT[c, o, :, cols]) + decode(RM[c, zh, :, cols])
                + decode(RP[c, zh, :, cols]) + decode(ZR[c, :, cols])
            )

        for h in (0, 1):
            if g is None or g == h:
                first, _, width = GROUPS[h]
                units = hidden_columns(h)
                gate = total(pl.ds(first, width)) * (gs[units] * (1.0 / LIFT))[None, :]
                up = total(pl.ds(first + width, width)) * (us[units] * (1.0 / LIFT))[None, :]
                H[c, o, :, units] = (jax.nn.silu(gate) * up).astype(BF)
        rows = H.at[c, o, :, hidden_columns(g)]
        send(rows, rows, ("h+", c, g), to_yp)
        send(rows, rows, ("h-", c, g), to_ym)
        send(rows, rows, ("hz", c, g), to_zh)
        if c in DIRECT + Z_FIRST:
            send(rows, rows, ("h2", c, g), to_y2)
        if c in DIRECT:
            send(rows, rows, ("hz+", c, g), to_zh_yp)
            send(rows, rows, ("hz-", c, g), to_zh_ym)
            send(rows, rows, ("hz2", c, g), to_zh_y2)

    def pass_on(c, g=None):
        rows = H.at[c, own(y, zo), :, hidden_columns(g)]
        arrived(rows, ("hz", c, g))
        send(rows, rows, ("hz+", c, g), to_yp)
        send(rows, rows, ("hz-", c, g), to_ym)
        send(rows, rows, ("hz2", c, g), to_y2)

    def near(c):
        rows = H.at[c, own(ym, zh)]
        arrived(rows, ("h+", c, None))
        left = rows.at[:, pl.ds(0, HALF)]
        send(left, left, ("hv+", c), to_yp)
        send(rows, rows, ("hz+", c, None), to_zh)
        rows = H.at[c, own(yp, zh)]
        arrived(rows, ("h-", c, None))
        right = rows.at[:, pl.ds(HALF, N - HALF)]
        send(right, right, ("hv-", c), to_ym)
        send(rows, rows, ("hz-", c, None), to_zh)

    def far(c):
        rows = H.at[c, own(y2, zh)]
        arrived(rows.at[:, pl.ds(0, HALF)], ("hv+", c))
        arrived(rows.at[:, pl.ds(HALF, N - HALF)], ("hv-", c))
        send(rows, rows, ("hz2", c, None), to_zh)

    def down_tile(c, n):
        cols = pl.ds(pl.multiple_of(n * 1024, 1024), 1024)
        rows = H[c].reshape(128, N)
        part = jnp.dot(rows, WD[:, cols], preferred_element_type=F32)
        D[c % 2, :, :, cols] = part.reshape(2, 64, 1024)

    def hidden_arrived(c, g):
        keys = [("hz", y, zo), ("hz+", ym, zo), ("hz-", yp, zo), ("hz2", y2, zo)]
        if c in Z_FIRST:
            keys = keys[1:]
        if c in DIRECT + Z_FIRST:
            keys += [("h+", ym, zh), ("h-", yp, zh), ("h2", y2, zh)]
        for key, y_, z_ in keys:
            arrived(H.at[c, own(y_, z_), :, hidden_columns(g)], (key, c, g))

    def before_down(c):
        if c == 0:
            wd_copy.wait()
        if c >= 2:
            on_way.pop(("core", c - 2)).wait_send()

    def down(c):
        hidden_arrived(c, None)
        before_down(c)

        def step(n, carry):
            down_tile(c, n)
            return carry

        lax.fori_loop(0, 2, step, 0)
        send(D.at[c % 2, other], CR.at[c], ("core", c), to_core)

    def down_first(c):
        hidden_arrived(c, 0)
        before_down(c)

        def step(n, carry):
            cols = pl.ds(pl.multiple_of(n * 1024, 1024), 1024)
            rows = H[c, :, :, pl.ds(0, 896)].reshape(128, 896)
            part = jnp.dot(rows, WD[pl.ds(0, 896), cols], preferred_element_type=F32)
            D[c % 2, :, :, cols] = part.reshape(2, 64, 1024)
            return carry

        lax.fori_loop(0, 2, step, 0)

    def down_rest(c, n):
        if n == 0:
            hidden_arrived(c, 1)
        cols = pl.ds(n * 1024, 1024)
        rows = H[c, :, :, pl.ds(896, 768)].reshape(128, 768)
        part = jnp.dot(rows, WD[pl.ds(896, 768), cols], preferred_element_type=F32)
        D[c % 2, :, :, cols] += part.reshape(2, 64, 1024)
        send(D.at[c % 2, other, :, cols], CR.at[c, :, cols], ("core", c, n), to_core)

    def add_cores(c, cols, tag):
        name = CHUNKS[c]
        arrived(CR.at[c, :, cols], ("core", c) + tag)
        total = D[c % 2, core, :, cols] + CR[c, :, cols]
        if name not in ALONG_X:
            ACC[("own", "z").index(name), :, cols] = total
            return
        XS[c, :, cols] = total.astype(BF)
        ways = ALONG_X[name]
        rows = 64 // len(ways)
        for i, d in enumerate(ways):
            part = pl.ds(i * rows, rows)
            send(XS.at[c, part, cols], XR.at[c, part, cols], ("x", c, i) + tag, to_x[d])

    def over_core(c):
        add_cores(c, pl.ds(0, M), ())

    def sums_arrived(c):
        ways = ALONG_X[CHUNKS[c]]
        rows = 64 // len(ways)
        for i in range(len(ways)):
            part = pl.ds(i * rows, rows)
            if c in SPLIT:
                for n in range(2):
                    cols = pl.ds(n * 1024, 1024)
                    arrived(XR.at[c, part, cols], ("x", c, i, n))
            else:
                arrived(XR.at[c, part], ("x", c, i))

    def partner(i):
        whole = CHUNKS.index("zx2")
        half = CHUNKS.index(("zmixA", "zmixB")[i])
        if i == 0:
            sums_arrived(whole)
        sums_arrived(half)
        rows = pl.ds(32 * i, 32)
        total = ACC[1, rows] + XR[whole, rows].astype(F32)
        total = total + XR[half, 0:32].astype(F32) + XR[half, 32:64].astype(F32)
        ZLB[rows] = total.astype(BF)
        send(ZLB.at[rows], ZLR.at[rows], ("z_lo", i), to_zl)

    own_key, z_key = ("fwd", CHUNKS.index("own")), ("tok", "z")
    send(tok, T.at[CHUNKS.index("own"), core], own_key, to_core)
    send(tok, T.at[CHUNKS.index("z"), core], z_key, to_zl)

    steps = dict(
        send_far=send_far, send_near=send_near, forward=forward, gate_up=gate_up, near_sums=near_sums, relay=relay, over_y=over_y,
        hidden=hidden, near=near, far=far, down=down, over_core=over_core, partner_a=lambda _: partner(0), partner_b=lambda _: partner(1),
        relay_a=lambda c: relay(c, 0), relay_b=lambda c: relay(c, 1),
        over_y_a=lambda c: over_y(c, 0), over_y_b=lambda c: over_y(c, 1),
        hidden_a=lambda c: hidden(c, 0), hidden_b=lambda c: hidden(c, 1),
        pass_on=pass_on, pass_on_a=lambda c: pass_on(c, 0), pass_on_b=lambda c: pass_on(c, 1),
        down_first=down_first, down_a=lambda c: down_rest(c, 0), down_b=lambda c: down_rest(c, 1),
        over_core_a=lambda c: add_cores(c, pl.ds(0, 1024), (0,)),
        over_core_b=lambda c: add_cores(c, pl.ds(1024, 1024), (1,)),
    )
    for name, c in ORDER:
        steps[name](c)

    for key in list(on_way):
        if key[0] not in ("x", "z_lo", "core") or (key[0] == "x" and key[1] not in SPLIT):
            on_way.pop(key).wait_send()

    c2, ca, cb = CHUNKS.index("x2"), CHUNKS.index("mixA"), CHUNKS.index("mixB")
    sums_arrived(c2)
    for i, c in enumerate((ca, cb)):
        rows = pl.ds(32 * i, 32)
        arrived(ZLR.at[rows], ("z_lo", i))
        total = ACC[0, rows] + XR[c2, rows].astype(F32) + ZLR[rows].astype(F32)
        sums_arrived(c)
        total = total + XR[c, 0:32].astype(F32) + XR[c, 32:64].astype(F32)
        out[rows, :] = (total * ds[...][None, :]).astype(BF)

    for c in on_way.values():
        c.wait_send()


def on_device(tokens, gate_weight, up_weight, gate_scale, up_scale, down_weight, down_scale):
    hbm, vmem = pl.BlockSpec(memory_space=pl.ANY), pl.BlockSpec(memory_space=pltpu.VMEM)
    return pl.pallas_call(
        body,
        name="gated_layer",
        out_shape=pltpu.VMEM((64, M), BF),
        in_specs=[hbm] * 7,
        out_specs=vmem,
        scratch_shapes=[
            pltpu.VMEM((N,), F32),
            pltpu.VMEM((N,), F32),
            pltpu.VMEM((M,), F32),
            pltpu.VMEM((K, N2), BF),
            pltpu.VMEM((N, M), BF),
            pltpu.VMEM((NC, 2, 64, K), BF),
            pltpu.VMEM((NC, 8, 16, N2), BF),
            pltpu.VMEM((NC, 2, 16, N2), BF),
            pltpu.VMEM((NC, 2, 16, N2), BF),
            pltpu.VMEM((NC, 2, 16, N2), BF),
            pltpu.VMEM((4, 16, N2), BF),
            pltpu.VMEM((NC, 16, N2), BF),
            pltpu.VMEM((NC, 8, 16, N), BF),
            pltpu.VMEM((2, 2, 64, M), F32),
            pltpu.VMEM((NC, 64, M), F32),
            pltpu.VMEM((NC, 64, M), BF),
            pltpu.VMEM((NC, 64, M), BF),
            pltpu.VMEM((2, 64, M), F32),
            pltpu.VMEM((64, M), BF),
            pltpu.VMEM((64, M), BF),
            pltpu.SemaphoreType.DMA((NSEM,)),
            pltpu.SemaphoreType.DMA((NSEM,)),
            pltpu.SemaphoreType.DMA((10,)),
        ],
        compiler_params=pltpu.CompilerParams(
            collective_id=0, has_side_effects=True, vmem_limit_bytes=62 * 2**20
        ),
        cost_estimate=pl.CostEstimate(
            flops=2 * 1024 * K * N2 + 2 * 1024 * N * M, bytes_accessed=2 * (K * N2 + N * M), transcendentals=0
        ),
    )(tokens, gate_weight, up_weight, gate_scale, up_scale, down_weight, down_scale)


def solution(mesh):
    return jax.shard_map(
        on_device,
        mesh=mesh,
        in_specs=(
            P("gy", "gx"),
            P("gx", "gy"),
            P("gx", "gy"),
            P("gy"),
            P("gy"),
            P("gy", "gx"),
            P("gx"),
        ),
        out_specs=P("gy", "gx"),
        check_vma=False,
    )
```

```python
import jax
import jax.numpy as jnp
from jax import lax
from jax.experimental import pallas as pl
from jax.experimental.pallas import tpu as pltpu
from jax.sharding import PartitionSpec as P

MESH = pl.DeviceIdType.MESH
BF, F32 = jnp.bfloat16, jnp.float32
NC = 8
K, N, N2, M = 2048, 1664, 3328, 2048
HALF = 896
LIFT = 2.0**50
TINY = 1e-37

CHUNKS = ("own", "z", "x2", "zx2", "zmixA", "zmixB", "mixA", "mixB")
DIRECT = (7,)
Z_SUMS_FIRST = (3,)
Z_FIRST = (6,)
SPLIT = (6, 7)
RS_GROUPS = (0, 6, 7)
(
    FORWARD, GATE_UP, NEAR_SUMS, RELAY, OVER_Y, HIDDEN, NEAR, FAR, DOWN, OVER_CORE, DOWN_A, DOWN_B, DOWN_FIRST,
    PASS_ON, PASS_ON_A, PASS_ON_B, RELAY_A, RELAY_B, OVER_Y_A, OVER_Y_B, HIDDEN_A, HIDDEN_B, OVER_CORE_A,
    OVER_CORE_B, PARTNER_A, PARTNER_B, SEND_FAR, SEND_NEAR,
) = range(28)
ORDER = (
    (SEND_FAR, 0), (GATE_UP, 0), (NEAR_SUMS, 0), (FORWARD, 1), (RELAY_A, 0), (FORWARD, 2), (RELAY_B, 0),
    (GATE_UP, 1), (NEAR_SUMS, 1), (OVER_Y, 0), (GATE_UP, 2), (FORWARD, 3), (SEND_NEAR, 0), (NEAR_SUMS, 2),
    (HIDDEN, 0), (FORWARD, 4), (GATE_UP, 3), (RELAY, 2), (RELAY, 1), (GATE_UP, 4), (NEAR, 0), (FORWARD, 5),
    (GATE_UP, 5), (NEAR_SUMS, 4), (FORWARD, 7), (RELAY, 4), (OVER_Y, 1), (OVER_Y, 2), (FAR, 0), (NEAR_SUMS, 3),
    (HIDDEN, 1), (OVER_Y, 4), (HIDDEN, 2), (RELAY, 3), (FORWARD, 6), (NEAR, 1), (RELAY, 5), (DOWN, 0), (HIDDEN, 4),
    (HIDDEN, 3), (FAR, 1), (NEAR, 2), (NEAR_SUMS, 5), (GATE_UP, 6), (NEAR, 3), (FAR, 2), (GATE_UP, 7), (OVER_Y, 5),
    (RELAY_A, 6), (DOWN, 1), (FAR, 3), (NEAR, 4), (NEAR_SUMS, 6), (OVER_CORE, 0), (RELAY_B, 6), (DOWN, 2), (FAR, 4),
    (HIDDEN, 5), (OVER_CORE, 1), (NEAR_SUMS, 7), (DOWN, 3), (OVER_Y_A, 6), (RELAY_A, 7), (OVER_CORE, 2),
    (OVER_Y_B, 6), (NEAR, 5), (RELAY_B, 7), (DOWN, 4), (HIDDEN_A, 6), (HIDDEN_B, 6), (OVER_Y_A, 7), (OVER_CORE, 3),
    (FAR, 5), (OVER_Y_B, 7), (OVER_CORE, 4), (PASS_ON_A, 6), (PASS_ON_B, 6), (HIDDEN_A, 7), (DOWN, 5), (HIDDEN_B, 7),
    (DOWN_FIRST, 6), (DOWN_A, 6), (OVER_CORE, 5), (PARTNER_A, 0), (OVER_CORE_A, 6), (DOWN_B, 6), (DOWN_FIRST, 7),
    (DOWN_A, 7), (DOWN_B, 7), (OVER_CORE_B, 6), (OVER_CORE_A, 7), (PARTNER_B, 0), (OVER_CORE_B, 7),
)

ALONG_X = {"x2": (2,), "zx1": (1,), "zx2": (2,), "zx3": (3,), "mixA": (1, 3), "mixB": (1, 3), "zmixA": (1, 3), "zmixB": (1, 3)}
PIECES = ((0, 0, 896, 0), (1, 0, 896, 896), (0, 896, 768, 1792), (1, 896, 768, 2560))
W_FOR_TILE = ((0, 1), (2,), (3,), ())
GROUPS = ((0, 0, 896), (1792, 896, 768))
NSEM = 208


def sum_columns(g):
    return pl.ds(0, N2) if g is None else pl.ds(GROUPS[g][0], 2 * GROUPS[g][2])


def hidden_columns(g):
    return pl.ds(0, N) if g is None else pl.ds(GROUPS[g][1], GROUPS[g][2])


def parts(c, chunks):
    return (0, 1) if c in chunks else (None,)


def encode(v):
    v = v * LIFT
    return (v * jnp.abs(v)).astype(BF)


def decode(q):
    q = q.astype(F32)
    return q * lax.rsqrt(jnp.maximum(jnp.abs(q), TINY))


def recode(s):
    return (s * jnp.abs(s)).astype(BF)


def body(tok, wg, wu, gs_in, us_in, wd, ds_in, out, gs, us, ds, W, WD, T, PT, RL, RM, RP, ZX, ZR, H, D, CR, XS, XR, ACC, ZLB, ZLR, ssem, rsem, lsem):
    gx, gy = lax.axis_index("gx"), lax.axis_index("gy")
    zh, y = gx // 4, lax.rem(gx, 4)
    zl, x, core = gy // 8, lax.rem(gy // 2, 4), lax.rem(gy, 2)
    zo, other = 1 - zh, 1 - core
    yp, ym, y2 = lax.rem(y + 1, 4), lax.rem(y + 3, 4), lax.rem(y + 2, 4)

    def at(zh_=zh, y_=y, zl_=zl, x_=x, core_=core):
        return (zh_ * 4 + y_, zl_ * 8 + x_ * 2 + core_)

    to_yp, to_ym, to_y2 = at(y_=yp), at(y_=ym), at(y_=y2)
    to_zh, to_zh_yp, to_zh_ym, to_zh_y2 = at(zh_=zo), at(zh_=zo, y_=yp), at(zh_=zo, y_=ym), at(zh_=zo, y_=y2)
    to_zl, to_core = at(zl_=1 - zl), at(core_=other)
    to_x = [None] + [at(x_=lax.rem(x + d, 4)) for d in (1, 2, 3)]

    def own(y_, z_):
        return y_ * 2 + z_

    semaphore, on_way = {}, {}

    def copy(src, dst, key, to):
        k = semaphore.setdefault(key, len(semaphore))
        return pltpu.make_async_remote_copy(
            src_ref=src, dst_ref=dst, send_sem=ssem.at[k], recv_sem=rsem.at[k], device_id=to, device_id_type=MESH
        )

    def send(src, dst, key, to):
        on_way[key] = copy(src, dst, key, to)
        on_way[key].start()

    def arrived(dst, key):
        copy(dst, dst, key, to_core).wait_recv()

    w_copies = [
        pltpu.make_async_copy((wg, wu)[m].at[:, pl.ds(c0, n)], W.at[:, pl.ds(d0, n)], lsem.at[i])
        for i, (m, c0, n, d0) in enumerate(PIECES)
    ]
    own_copy = pltpu.make_async_copy(tok, T.at[CHUNKS.index("own"), core], lsem.at[5])
    wd_copy = pltpu.make_async_copy(wd, WD, lsem.at[6])
    scale_copies = [
        pltpu.make_async_copy(a, b, lsem.at[7 + i]) for i, (a, b) in enumerate(((gs_in, gs), (us_in, us), (ds_in, ds)))
    ]
    own_copy.start()
    for c in w_copies + scale_copies:
        c.start()

    barrier = pltpu.get_barrier_semaphore()
    partners = [to_yp, to_ym, to_y2, to_zh, to_zh_yp, to_zh_ym, to_zh_y2, to_zl, to_core] + to_x[1:]
    for p in partners:
        pl.semaphore_signal(barrier, inc=1, device_id=p, device_id_type=MESH)
    pl.semaphore_wait(barrier, len(partners))

    def chunk_tokens(c):
        name = CHUNKS[c]
        if "mix" in name:
            return [(T.at[c, core, pl.ds(32 * i, 32)], ("tok", name, d)) for i, d in enumerate((1, 3))]
        return [(T.at[c, core], ("tok", name))]

    def send_far(_):
        send(tok, T.at[CHUNKS.index("x2"), core], ("tok", "x2"), to_x[2])

    def mixed(rows, name):
        c = CHUNKS.index(name)
        rows = rows.at[pl.ds(32 * "AB".index(name[-1]), 32)]
        send(rows, T.at[c, core, pl.ds(32, 32)], ("tok", name, 3), to_x[1])
        send(rows, T.at[c, core, pl.ds(0, 32)], ("tok", name, 1), to_x[3])

    def send_near(_):
        mixed(tok, "mixA")
        mixed(tok, "mixB")

    def forward(c):
        for where, key in chunk_tokens(c):
            arrived(where, key)
        send(T.at[c, core], T.at[c, core], ("fwd", c), to_core)
        if CHUNKS[c] == "z":
            for name in CHUNKS:
                if name[:2] == "zx":
                    send(T.at[c, core], T.at[CHUNKS.index(name), core], ("tok", name), to_x[4 - int(name[2])])
                if name[:4] == "zmix":
                    mixed(T.at[c, core], name)

    def gate_up(c):
        if CHUNKS[c] == "own":
            own_copy.wait()
        arrived(T.at[c, other], ("fwd", c))

        def tile(n0, width):
            rows = T[c].reshape(128, K)
            part = jnp.dot(rows, W[:, pl.ds(n0, width)], preferred_element_type=F32)
            PT[c, :, :, pl.ds(n0, width)] = encode(part).reshape(8, 16, width)

        def far_sums(g):
            cols = sum_columns(g)
            send(PT.at[c, own(y2, 0), :, cols], RL.at[c, 0, :, cols], ("far+", c, g), to_yp)
            send(PT.at[c, own(y2, 1), :, cols], RL.at[c, 1, :, cols], ("far-", c, g), to_ym)

        if c == 0:
            for t in range(2):
                for i in W_FOR_TILE[t]:
                    w_copies[i].wait()
                tile(1024 * t, 1024)
            if c in RS_GROUPS:
                far_sums(0)
            w_copies[3].wait()
            tile(2048, 1024)
        else:

            def step(n, carry):
                tile(pl.multiple_of(n * 1024, 1024), 1024)
                return carry

            lax.fori_loop(0, 3, step, 0)
        tile(3072, 256)
        if c in Z_SUMS_FIRST:
            for j in range(4):
                send(PT.at[c, own(j, zo)], ZX.at[j], ("z_first", c, j), to_zh)
        else:
            for g in parts(c, RS_GROUPS):
                if c or g != 0:
                    far_sums(g)
        if c == 0:
            wd_copy.start()

    def z_sums(c):
        for j in range(4):
            arrived(ZX.at[j], ("z_first", c, j))
        a, b = sum_columns(0), sum_columns(1)

        def add(y_):
            o = own(y_, zh)
            PT[c, o] = recode(decode(PT[c, o]) + decode(ZX[y_]))
            return PT.at[c, o]

        far = add(y2)
        send(far.at[:, a], RL.at[c, 0, :, a], ("far+", c), to_yp)
        send(far.at[:, b], RL.at[c, 1, :, b], ("far-", c), to_ym)
        send(add(yp).at[:, b], RM.at[c, 0, :, b], ("near+", c), to_yp)
        send(add(ym).at[:, a], RP.at[c, 0, :, a], ("near-", c), to_ym)
        add(y)

    def relay_z_sums(c):
        for i, (y_, g, dst, far, via, to) in enumerate(
            ((yp, 0, RM, "far+", "via+", to_yp), (ym, 1, RP, "far-", "via-", to_ym))
        ):
            o, cols = own(y_, zh), sum_columns(g)
            arrived(RL.at[c, i, :, cols], (far, c))
            PT[c, o, :, cols] = recode(decode(PT[c, o, :, cols]) + decode(RL[c, i, :, cols]))
            send(PT.at[c, o, :, cols], dst.at[c, 0, :, cols], (via, c), to)

    def near_sums(c):
        if c in Z_SUMS_FIRST:
            z_sums(c)
            return
        if c == 0:
            for scale in scale_copies:
                scale.wait()
        for g in parts(c, RS_GROUPS):
            cols = sum_columns(g)
            send(PT.at[c, own(yp, 1), :, cols], RM.at[c, 1, :, cols], ("near+", c, g), to_yp)
            send(PT.at[c, own(ym, 0), :, cols], RP.at[c, 0, :, cols], ("near-", c, g), to_ym)

    def relay(c, g=None):
        if c in Z_SUMS_FIRST:
            relay_z_sums(c)
            return
        cols = sum_columns(g)
        for i, (o, dst, far, via, to) in enumerate(
            ((own(yp, 0), RM, "far+", "via+", to_yp), (own(ym, 1), RP, "far-", "via-", to_ym))
        ):
            arrived(RL.at[c, i, :, cols], (far, c, g))
            PT[c, o, :, cols] = recode(decode(PT[c, o, :, cols]) + decode(RL[c, i, :, cols]))
            send(PT.at[c, o, :, cols], dst.at[c, i, :, cols], (via, c, g), to)

    def over_y(c, g=None):
        for h in parts(c, RS_GROUPS):
            if g is None or g == h:
                cols = sum_columns(h)
                arrived(RM.at[c, 1, :, cols], ("near+", c, h))
                arrived(RP.at[c, 0, :, cols], ("near-", c, h))
                arrived(RM.at[c, 0, :, cols], ("via+", c, h))
                arrived(RP.at[c, 1, :, cols], ("via-", c, h))
        o, cols = own(y, zo), sum_columns(g)
        PT[c, o, :, cols] = recode(
            decode(PT[c, o, :, cols]) + decode(RM[c, zo, :, cols]) + decode(RP[c, zo, :, cols])
        )
        send(PT.at[c, o, :, cols], ZR.at[c, :, cols], ("z_hi", c, g), to_zh)

    def hidden(c, g=None):
        o = own(y, zh)
        if c in Z_SUMS_FIRST:
            for h, plus, minus in ((0, "via+", "near-"), (1, "near+", "via-")):
                arrived(RM.at[c, 0, :, sum_columns(h)], (plus, c))
                arrived(RP.at[c, 0, :, sum_columns(h)], (minus, c))
        else:
            arrived(ZR.at[c, :, sum_columns(g)], ("z_hi", c, g))

        def total(cols):
            if c in Z_SUMS_FIRST:
                return decode(PT[c, o, :, cols]) + decode(RM[c, 0, :, cols]) + decode(RP[c, 0, :, cols])
            return (
                decode(PT[c, o, :, cols]) + decode(RM[c, zh, :, cols])
                + decode(RP[c, zh, :, cols]) + decode(ZR[c, :, cols])
            )

        for h in (0, 1):
            if g is None or g == h:
                first, _, width = GROUPS[h]
                units = hidden_columns(h)
                gate = total(pl.ds(first, width)) * (gs[units] * (1.0 / LIFT))[None, :]
                up = total(pl.ds(first + width, width)) * (us[units] * (1.0 / LIFT))[None, :]
                H[c, o, :, units] = (jax.nn.silu(gate) * up).astype(BF)
        rows = H.at[c, o, :, hidden_columns(g)]
        send(rows, rows, ("h+", c, g), to_yp)
        send(rows, rows, ("h-", c, g), to_ym)
        send(rows, rows, ("hz", c, g), to_zh)
        if c in DIRECT + Z_FIRST:
            send(rows, rows, ("h2", c, g), to_y2)
        if c in DIRECT:
            send(rows, rows, ("hz+", c, g), to_zh_yp)
            send(rows, rows, ("hz-", c, g), to_zh_ym)
            send(rows, rows, ("hz2", c, g), to_zh_y2)

    def pass_on(c, g=None):
        rows = H.at[c, own(y, zo), :, hidden_columns(g)]
        arrived(rows, ("hz", c, g))
        send(rows, rows, ("hz+", c, g), to_yp)
        send(rows, rows, ("hz-", c, g), to_ym)
        send(rows, rows, ("hz2", c, g), to_y2)

    def near(c):
        rows = H.at[c, own(ym, zh)]
        arrived(rows, ("h+", c, None))
        left = rows.at[:, pl.ds(0, HALF)]
        send(left, left, ("hv+", c), to_yp)
        send(rows, rows, ("hz+", c, None), to_zh)
        rows = H.at[c, own(yp, zh)]
        arrived(rows, ("h-", c, None))
        right = rows.at[:, pl.ds(HALF, N - HALF)]
        send(right, right, ("hv-", c), to_ym)
        send(rows, rows, ("hz-", c, None), to_zh)

    def far(c):
        rows = H.at[c, own(y2, zh)]
        arrived(rows.at[:, pl.ds(0, HALF)], ("hv+", c))
        arrived(rows.at[:, pl.ds(HALF, N - HALF)], ("hv-", c))
        send(rows, rows, ("hz2", c, None), to_zh)

    def down_tile(c, n):
        cols = pl.ds(pl.multiple_of(n * 1024, 1024), 1024)
        rows = H[c].reshape(128, N)
        part = jnp.dot(rows, WD[:, cols], preferred_element_type=F32)
        D[c % 2, :, :, cols] = part.reshape(2, 64, 1024)

    def hidden_arrived(c, g):
        keys = [("hz", y, zo), ("hz+", ym, zo), ("hz-", yp, zo), ("hz2", y2, zo)]
        if c in Z_FIRST:
            keys = keys[1:]
        if c in DIRECT + Z_FIRST:
            keys += [("h+", ym, zh), ("h-", yp, zh), ("h2", y2, zh)]
        for key, y_, z_ in keys:
            arrived(H.at[c, own(y_, z_), :, hidden_columns(g)], (key, c, g))

    def before_down(c):
        if c == 0:
            wd_copy.wait()
        if c >= 2:
            on_way.pop(("core", c - 2)).wait_send()

    def down(c):
        hidden_arrived(c, None)
        before_down(c)

        def step(n, carry):
            down_tile(c, n)
            return carry

        lax.fori_loop(0, 2, step, 0)
        send(D.at[c % 2, other], CR.at[c], ("core", c), to_core)

    def down_first(c):
        hidden_arrived(c, 0)
        before_down(c)

        def step(n, carry):
            cols = pl.ds(pl.multiple_of(n * 1024, 1024), 1024)
            rows = H[c, :, :, pl.ds(0, 896)].reshape(128, 896)
            part = jnp.dot(rows, WD[pl.ds(0, 896), cols], preferred_element_type=F32)
            D[c % 2, :, :, cols] = part.reshape(2, 64, 1024)
            return carry

        lax.fori_loop(0, 2, step, 0)

    def down_rest(c, n):
        if n == 0:
            hidden_arrived(c, 1)
        cols = pl.ds(n * 1024, 1024)
        rows = H[c, :, :, pl.ds(896, 768)].reshape(128, 768)
        part = jnp.dot(rows, WD[pl.ds(896, 768), cols], preferred_element_type=F32)
        D[c % 2, :, :, cols] += part.reshape(2, 64, 1024)
        send(D.at[c % 2, other, :, cols], CR.at[c, :, cols], ("core", c, n), to_core)

    def add_cores(c, cols, tag):
        name = CHUNKS[c]
        arrived(CR.at[c, :, cols], ("core", c) + tag)
        total = D[c % 2, core, :, cols] + CR[c, :, cols]
        if name not in ALONG_X:
            ACC[("own", "z").index(name), :, cols] = total
            return
        XS[c, :, cols] = total.astype(BF)
        ways = ALONG_X[name]
        rows = 64 // len(ways)
        for i, d in enumerate(ways):
            part = pl.ds(i * rows, rows)
            send(XS.at[c, part, cols], XR.at[c, part, cols], ("x", c, i) + tag, to_x[d])

    def over_core(c):
        add_cores(c, pl.ds(0, M), ())

    def sums_arrived(c):
        ways = ALONG_X[CHUNKS[c]]
        rows = 64 // len(ways)
        for i in range(len(ways)):
            part = pl.ds(i * rows, rows)
            if c in SPLIT:
                for n in range(2):
                    cols = pl.ds(n * 1024, 1024)
                    arrived(XR.at[c, part, cols], ("x", c, i, n))
            else:
                arrived(XR.at[c, part], ("x", c, i))

    def partner(i):
        whole = CHUNKS.index("zx2")
        half = CHUNKS.index(("zmixA", "zmixB")[i])
        if i == 0:
            sums_arrived(whole)
        sums_arrived(half)
        rows = pl.ds(32 * i, 32)
        total = ACC[1, rows] + XR[whole, rows].astype(F32)
        total = total + XR[half, 0:32].astype(F32) + XR[half, 32:64].astype(F32)
        ZLB[rows] = total.astype(BF)
        send(ZLB.at[rows], ZLR.at[rows], ("z_lo", i), to_zl)

    own_key, z_key = ("fwd", CHUNKS.index("own")), ("tok", "z")
    send(tok, T.at[CHUNKS.index("own"), core], own_key, to_core)
    send(tok, T.at[CHUNKS.index("z"), core], z_key, to_zl)

    steps = {
        SEND_FAR: send_far, SEND_NEAR: send_near, FORWARD: forward, GATE_UP: gate_up, NEAR_SUMS: near_sums,
        RELAY: relay, RELAY_A: lambda c: relay(c, 0), RELAY_B: lambda c: relay(c, 1),
        OVER_Y: over_y, OVER_Y_A: lambda c: over_y(c, 0), OVER_Y_B: lambda c: over_y(c, 1),
        HIDDEN: hidden, HIDDEN_A: lambda c: hidden(c, 0), HIDDEN_B: lambda c: hidden(c, 1),
        NEAR: near, FAR: far, PASS_ON: pass_on, PASS_ON_A: lambda c: pass_on(c, 0), PASS_ON_B: lambda c: pass_on(c, 1),
        DOWN: down, DOWN_FIRST: down_first, DOWN_A: lambda c: down_rest(c, 0), DOWN_B: lambda c: down_rest(c, 1),
        OVER_CORE: over_core,
        OVER_CORE_A: lambda c: add_cores(c, pl.ds(0, 1024), (0,)),
        OVER_CORE_B: lambda c: add_cores(c, pl.ds(1024, 1024), (1,)),
        PARTNER_A: lambda _: partner(0), PARTNER_B: lambda _: partner(1),
    }
    for name, c in ORDER:
        steps[name](c)

    for key in list(on_way):
        if key[0] not in ("x", "z_lo", "core") or (key[0] == "x" and key[1] not in SPLIT):
            on_way.pop(key).wait_send()

    c2, ca, cb = CHUNKS.index("x2"), CHUNKS.index("mixA"), CHUNKS.index("mixB")
    sums_arrived(c2)
    for i, c in enumerate((ca, cb)):
        rows = pl.ds(32 * i, 32)
        arrived(ZLR.at[rows], ("z_lo", i))
        total = ACC[0, rows] + XR[c2, rows].astype(F32) + ZLR[rows].astype(F32)
        sums_arrived(c)
        total = total + XR[c, 0:32].astype(F32) + XR[c, 32:64].astype(F32)
        out[rows, :] = (total * ds[...][None, :]).astype(BF)

    for c in on_way.values():
        c.wait_send()


def on_device(tokens, gate_weight, up_weight, gate_scale, up_scale, down_weight, down_scale):
    hbm, vmem = pl.BlockSpec(memory_space=pl.ANY), pl.BlockSpec(memory_space=pltpu.VMEM)
    return pl.pallas_call(
        body,
        name="gated_layer",
        out_shape=pltpu.VMEM((64, M), BF),
        in_specs=[hbm] * 7,
        out_specs=vmem,
        scratch_shapes=[
            pltpu.VMEM((N,), F32),
            pltpu.VMEM((N,), F32),
            pltpu.VMEM((M,), F32),
            pltpu.VMEM((K, N2), BF),
            pltpu.VMEM((N, M), BF),
            pltpu.VMEM((NC, 2, 64, K), BF),
            pltpu.VMEM((NC, 8, 16, N2), BF),
            pltpu.VMEM((NC, 2, 16, N2), BF),
            pltpu.VMEM((NC, 2, 16, N2), BF),
            pltpu.VMEM((NC, 2, 16, N2), BF),
            pltpu.VMEM((4, 16, N2), BF),
            pltpu.VMEM((NC, 16, N2), BF),
            pltpu.VMEM((NC, 8, 16, N), BF),
            pltpu.VMEM((2, 2, 64, M), F32),
            pltpu.VMEM((NC, 64, M), F32),
            pltpu.VMEM((NC, 64, M), BF),
            pltpu.VMEM((NC, 64, M), BF),
            pltpu.VMEM((2, 64, M), F32),
            pltpu.VMEM((64, M), BF),
            pltpu.VMEM((64, M), BF),
            pltpu.SemaphoreType.DMA((NSEM,)),
            pltpu.SemaphoreType.DMA((NSEM,)),
            pltpu.SemaphoreType.DMA((10,)),
        ],
        compiler_params=pltpu.CompilerParams(
            collective_id=0, has_side_effects=True, vmem_limit_bytes=62 * 2**20
        ),
        cost_estimate=pl.CostEstimate(
            flops=2 * 1024 * K * N2 + 2 * 1024 * N * M, bytes_accessed=2 * (K * N2 + N * M), transcendentals=0
        ),
    )(tokens, gate_weight, up_weight, gate_scale, up_scale, down_weight, down_scale)


def solution(mesh):
    return jax.shard_map(
        on_device,
        mesh=mesh,
        in_specs=(
            P("gy", "gx"),
            P("gx", "gy"),
            P("gx", "gy"),
            P("gy"),
            P("gy"),
            P("gy", "gx"),
            P("gx"),
        ),
        out_specs=P("gy", "gx"),
        check_vma=False,
    )
```

```python
import jax
import jax.numpy as jnp
from jax import lax
from jax.experimental import pallas as pl
from jax.experimental.pallas import tpu as pltpu
from jax.sharding import PartitionSpec as P

MESH = pl.DeviceIdType.MESH
BF, F32 = jnp.bfloat16, jnp.float32
NC = 8
K, N, N2, M = 2048, 1664, 3328, 2048
HALF = 896
LIFT = 2.0**50
TINY = 1e-37

CHUNKS = ("own", "z", "x2", "zx2", "zmixA", "zmixB", "mixA", "mixB")
DIRECT = (7,)
Z_SUMS_FIRST = (3,)
Z_FIRST = (6,)
SPLIT = (6, 7)
RS_GROUPS = (0, 6, 7)
(
    FORWARD, GATE_UP, NEAR_SUMS, RELAY, OVER_Y, HIDDEN, NEAR, FAR, DOWN, OVER_CORE, DOWN_A, DOWN_B, DOWN_FIRST,
    PASS_ON, PASS_ON_A, PASS_ON_B, RELAY_A, RELAY_B, OVER_Y_A, OVER_Y_B, HIDDEN_A, HIDDEN_B, OVER_CORE_A,
    OVER_CORE_B, PARTNER_A, PARTNER_B, SEND_FAR, SEND_NEAR,
) = range(28)
ORDER = (
    (SEND_FAR, 0), (GATE_UP, 0), (NEAR_SUMS, 0), (FORWARD, 1), (RELAY_A, 0), (FORWARD, 2), (RELAY_B, 0),
    (GATE_UP, 1), (NEAR_SUMS, 1), (OVER_Y, 0), (GATE_UP, 2), (FORWARD, 3), (SEND_NEAR, 0), (NEAR_SUMS, 2),
    (HIDDEN, 0), (FORWARD, 4), (GATE_UP, 3), (RELAY, 2), (RELAY, 1), (GATE_UP, 4), (NEAR, 0), (FORWARD, 5),
    (GATE_UP, 5), (NEAR_SUMS, 4), (FORWARD, 7), (RELAY, 4), (OVER_Y, 1), (OVER_Y, 2), (FAR, 0), (NEAR_SUMS, 3),
    (HIDDEN, 1), (OVER_Y, 4), (HIDDEN, 2), (RELAY, 3), (FORWARD, 6), (NEAR, 1), (RELAY, 5), (DOWN, 0), (HIDDEN, 4),
    (HIDDEN, 3), (FAR, 1), (NEAR, 2), (NEAR_SUMS, 5), (GATE_UP, 6), (NEAR, 3), (FAR, 2), (GATE_UP, 7), (OVER_Y, 5),
    (RELAY_A, 6), (DOWN, 1), (FAR, 3), (NEAR, 4), (NEAR_SUMS, 6), (OVER_CORE, 0), (RELAY_B, 6), (DOWN, 2), (FAR, 4),
    (HIDDEN, 5), (OVER_CORE, 1), (NEAR_SUMS, 7), (DOWN, 3), (OVER_Y_A, 6), (RELAY_A, 7), (OVER_CORE, 2),
    (OVER_Y_B, 6), (NEAR, 5), (RELAY_B, 7), (DOWN, 4), (HIDDEN_A, 6), (HIDDEN_B, 6), (OVER_Y_A, 7), (OVER_CORE, 3),
    (FAR, 5), (OVER_Y_B, 7), (OVER_CORE, 4), (PASS_ON_A, 6), (PASS_ON_B, 6), (HIDDEN_A, 7), (DOWN, 5), (HIDDEN_B, 7),
    (DOWN_FIRST, 6), (DOWN_A, 6), (OVER_CORE, 5), (PARTNER_A, 0), (OVER_CORE_A, 6), (DOWN_B, 6), (DOWN_FIRST, 7),
    (DOWN_A, 7), (DOWN_B, 7), (OVER_CORE_B, 6), (OVER_CORE_A, 7), (PARTNER_B, 0), (OVER_CORE_B, 7),
)

ALONG_X = {"x2": (2,), "zx1": (1,), "zx2": (2,), "zx3": (3,), "mixA": (1, 3), "mixB": (1, 3), "zmixA": (1, 3), "zmixB": (1, 3)}
PIECES = ((0, 0, 896, 0), (1, 0, 896, 896), (0, 896, 768, 1792), (1, 896, 768, 2560))
W_FOR_TILE = ((0, 1), (2,), (3,), ())
GROUPS = ((0, 0, 896), (1792, 896, 768))
NSEM = 208


def sum_columns(g):
    return pl.ds(0, N2) if g is None else pl.ds(GROUPS[g][0], 2 * GROUPS[g][2])


def hidden_columns(g):
    return pl.ds(0, N) if g is None else pl.ds(GROUPS[g][1], GROUPS[g][2])


def parts(c, chunks):
    return (0, 1) if c in chunks else (None,)


def encode(v):
    v = v * LIFT
    return (v * jnp.abs(v)).astype(BF)


def decode(q):
    q = q.astype(F32)
    return q * lax.rsqrt(jnp.maximum(jnp.abs(q), TINY))


def recode(s):
    return (s * jnp.abs(s)).astype(BF)


def body(tok, wg, wu, gs_in, us_in, wd, ds_in, out, gs, us, ds, W, WD, T, PT, RL, RM, RP, ZX, ZR, H, D, CR, XS, XR, ACC, ZLB, ZLR, ssem, rsem, lsem):
    gx, gy = lax.axis_index("gx"), lax.axis_index("gy")
    zh, y = gx // 4, lax.rem(gx, 4)
    zl, x, core = gy // 8, lax.rem(gy // 2, 4), lax.rem(gy, 2)
    zo, other = 1 - zh, 1 - core
    yp, ym, y2 = lax.rem(y + 1, 4), lax.rem(y + 3, 4), lax.rem(y + 2, 4)

    def at(zh_=zh, y_=y, zl_=zl, x_=x, core_=core):
        return (zh_ * 4 + y_, zl_ * 8 + x_ * 2 + core_)

    to_yp, to_ym, to_y2 = at(y_=yp), at(y_=ym), at(y_=y2)
    to_zh, to_zh_yp, to_zh_ym, to_zh_y2 = at(zh_=zo), at(zh_=zo, y_=yp), at(zh_=zo, y_=ym), at(zh_=zo, y_=y2)
    to_zl, to_core = at(zl_=1 - zl), at(core_=other)
    to_x = [None] + [at(x_=lax.rem(x + d, 4)) for d in (1, 2, 3)]

    def own(y_, z_):
        return y_ * 2 + z_

    semaphore, on_way = {}, {}

    def copy(src, dst, key, to):
        k = semaphore.setdefault(key, len(semaphore))
        return pltpu.make_async_remote_copy(
            src_ref=src, dst_ref=dst, send_sem=ssem.at[k], recv_sem=rsem.at[k], device_id=to, device_id_type=MESH
        )

    def send(src, dst, key, to):
        on_way[key] = copy(src, dst, key, to)
        on_way[key].start()

    def arrived(dst, key):
        copy(dst, dst, key, to_core).wait_recv()

    w_copies = [
        pltpu.make_async_copy((wg, wu)[m].at[:, pl.ds(c0, n)], W.at[:, pl.ds(d0, n)], lsem.at[i])
        for i, (m, c0, n, d0) in enumerate(PIECES)
    ]
    own_copy = pltpu.make_async_copy(tok, T.at[CHUNKS.index("own"), core], lsem.at[5])
    wd_copy = pltpu.make_async_copy(wd, WD, lsem.at[6])
    scale_copies = [
        pltpu.make_async_copy(a, b, lsem.at[7 + i]) for i, (a, b) in enumerate(((gs_in, gs), (us_in, us), (ds_in, ds)))
    ]
    own_copy.start()
    for c in w_copies + scale_copies:
        c.start()

    barrier = pltpu.get_barrier_semaphore()
    partners = [to_yp, to_ym, to_y2, to_zh, to_zh_yp, to_zh_ym, to_zh_y2, to_zl, to_core] + to_x[1:]
    for p in partners:
        pl.semaphore_signal(barrier, inc=1, device_id=p, device_id_type=MESH)
    pl.semaphore_wait(barrier, len(partners))
    own_copy.wait()
    mine = T.at[CHUNKS.index("own"), core]

    def chunk_tokens(c):
        name = CHUNKS[c]
        if "mix" in name:
            return [(T.at[c, core, pl.ds(32 * i, 32)], ("tok", name, d)) for i, d in enumerate((1, 3))]
        return [(T.at[c, core], ("tok", name))]

    def send_far(_):
        send(mine, T.at[CHUNKS.index("x2"), core], ("tok", "x2"), to_x[2])

    def mixed(rows, name):
        c = CHUNKS.index(name)
        rows = rows.at[pl.ds(32 * "AB".index(name[-1]), 32)]
        send(rows, T.at[c, core, pl.ds(32, 32)], ("tok", name, 3), to_x[1])
        send(rows, T.at[c, core, pl.ds(0, 32)], ("tok", name, 1), to_x[3])

    def send_near(_):
        mixed(mine, "mixA")
        mixed(mine, "mixB")

    def forward(c):
        for where, key in chunk_tokens(c):
            arrived(where, key)
        send(T.at[c, core], T.at[c, core], ("fwd", c), to_core)
        if CHUNKS[c] == "z":
            for name in CHUNKS:
                if name[:2] == "zx":
                    send(T.at[c, core], T.at[CHUNKS.index(name), core], ("tok", name), to_x[4 - int(name[2])])
                if name[:4] == "zmix":
                    mixed(T.at[c, core], name)

    def gate_up(c):
        arrived(T.at[c, other], ("fwd", c))

        def tile(n0, width):
            rows = T[c].reshape(128, K)
            part = jnp.dot(rows, W[:, pl.ds(n0, width)], preferred_element_type=F32)
            PT[c, :, :, pl.ds(n0, width)] = encode(part).reshape(8, 16, width)

        def far_sums(g):
            cols = sum_columns(g)
            send(PT.at[c, own(y2, 0), :, cols], RL.at[c, 0, :, cols], ("far+", c, g), to_yp)
            send(PT.at[c, own(y2, 1), :, cols], RL.at[c, 1, :, cols], ("far-", c, g), to_ym)

        if c == 0:
            for t in range(2):
                for i in W_FOR_TILE[t]:
                    w_copies[i].wait()
                tile(1024 * t, 1024)
            if c in RS_GROUPS:
                far_sums(0)
            w_copies[3].wait()
            tile(2048, 1024)
        else:

            def step(n, carry):
                tile(pl.multiple_of(n * 1024, 1024), 1024)
                return carry

            lax.fori_loop(0, 3, step, 0)
        tile(3072, 256)
        if c in Z_SUMS_FIRST:
            for j in range(4):
                send(PT.at[c, own(j, zo)], ZX.at[j], ("z_first", c, j), to_zh)
        else:
            for g in parts(c, RS_GROUPS):
                if c or g != 0:
                    far_sums(g)
        if c == 0:
            wd_copy.start()

    def z_sums(c):
        for j in range(4):
            arrived(ZX.at[j], ("z_first", c, j))
        a, b = sum_columns(0), sum_columns(1)

        def add(y_):
            o = own(y_, zh)
            PT[c, o] = recode(decode(PT[c, o]) + decode(ZX[y_]))
            return PT.at[c, o]

        far = add(y2)
        send(far.at[:, a], RL.at[c, 0, :, a], ("far+", c), to_yp)
        send(far.at[:, b], RL.at[c, 1, :, b], ("far-", c), to_ym)
        send(add(yp).at[:, b], RM.at[c, 0, :, b], ("near+", c), to_yp)
        send(add(ym).at[:, a], RP.at[c, 0, :, a], ("near-", c), to_ym)
        add(y)

    def relay_z_sums(c):
        for i, (y_, g, dst, far, via, to) in enumerate(
            ((yp, 0, RM, "far+", "via+", to_yp), (ym, 1, RP, "far-", "via-", to_ym))
        ):
            o, cols = own(y_, zh), sum_columns(g)
            arrived(RL.at[c, i, :, cols], (far, c))
            PT[c, o, :, cols] = recode(decode(PT[c, o, :, cols]) + decode(RL[c, i, :, cols]))
            send(PT.at[c, o, :, cols], dst.at[c, 0, :, cols], (via, c), to)

    def near_sums(c):
        if c in Z_SUMS_FIRST:
            z_sums(c)
            return
        if c == 0:
            for scale in scale_copies:
                scale.wait()
        for g in parts(c, RS_GROUPS):
            cols = sum_columns(g)
            send(PT.at[c, own(yp, 1), :, cols], RM.at[c, 1, :, cols], ("near+", c, g), to_yp)
            send(PT.at[c, own(ym, 0), :, cols], RP.at[c, 0, :, cols], ("near-", c, g), to_ym)

    def relay(c, g=None):
        if c in Z_SUMS_FIRST:
            relay_z_sums(c)
            return
        cols = sum_columns(g)
        for i, (o, dst, far, via, to) in enumerate(
            ((own(yp, 0), RM, "far+", "via+", to_yp), (own(ym, 1), RP, "far-", "via-", to_ym))
        ):
            arrived(RL.at[c, i, :, cols], (far, c, g))
            PT[c, o, :, cols] = recode(decode(PT[c, o, :, cols]) + decode(RL[c, i, :, cols]))
            send(PT.at[c, o, :, cols], dst.at[c, i, :, cols], (via, c, g), to)

    def over_y(c, g=None):
        for h in parts(c, RS_GROUPS):
            if g is None or g == h:
                cols = sum_columns(h)
                arrived(RM.at[c, 1, :, cols], ("near+", c, h))
                arrived(RP.at[c, 0, :, cols], ("near-", c, h))
                arrived(RM.at[c, 0, :, cols], ("via+", c, h))
                arrived(RP.at[c, 1, :, cols], ("via-", c, h))
        o, cols = own(y, zo), sum_columns(g)
        PT[c, o, :, cols] = recode(
            decode(PT[c, o, :, cols]) + decode(RM[c, zo, :, cols]) + decode(RP[c, zo, :, cols])
        )
        send(PT.at[c, o, :, cols], ZR.at[c, :, cols], ("z_hi", c, g), to_zh)

    def hidden(c, g=None):
        o = own(y, zh)
        if c in Z_SUMS_FIRST:
            for h, plus, minus in ((0, "via+", "near-"), (1, "near+", "via-")):
                arrived(RM.at[c, 0, :, sum_columns(h)], (plus, c))
                arrived(RP.at[c, 0, :, sum_columns(h)], (minus, c))
        else:
            arrived(ZR.at[c, :, sum_columns(g)], ("z_hi", c, g))

        def total(cols):
            if c in Z_SUMS_FIRST:
                return decode(PT[c, o, :, cols]) + decode(RM[c, 0, :, cols]) + decode(RP[c, 0, :, cols])
            return (
                decode(PT[c, o, :, cols]) + decode(RM[c, zh, :, cols])
                + decode(RP[c, zh, :, cols]) + decode(ZR[c, :, cols])
            )

        for h in (0, 1):
            if g is None or g == h:
                first, _, width = GROUPS[h]
                units = hidden_columns(h)
                gate = total(pl.ds(first, width)) * (gs[units] * (1.0 / LIFT))[None, :]
                up = total(pl.ds(first + width, width)) * (us[units] * (1.0 / LIFT))[None, :]
                H[c, o, :, units] = (jax.nn.silu(gate) * up).astype(BF)
        rows = H.at[c, o, :, hidden_columns(g)]
        send(rows, rows, ("h+", c, g), to_yp)
        send(rows, rows, ("h-", c, g), to_ym)
        send(rows, rows, ("hz", c, g), to_zh)
        if c in DIRECT + Z_FIRST:
            send(rows, rows, ("h2", c, g), to_y2)
        if c in DIRECT:
            send(rows, rows, ("hz+", c, g), to_zh_yp)
            send(rows, rows, ("hz-", c, g), to_zh_ym)
            send(rows, rows, ("hz2", c, g), to_zh_y2)

    def pass_on(c, g=None):
        rows = H.at[c, own(y, zo), :, hidden_columns(g)]
        arrived(rows, ("hz", c, g))
        send(rows, rows, ("hz+", c, g), to_yp)
        send(rows, rows, ("hz-", c, g), to_ym)
        send(rows, rows, ("hz2", c, g), to_y2)

    def near(c):
        rows = H.at[c, own(ym, zh)]
        arrived(rows, ("h+", c, None))
        left = rows.at[:, pl.ds(0, HALF)]
        send(left, left, ("hv+", c), to_yp)
        send(rows, rows, ("hz+", c, None), to_zh)
        rows = H.at[c, own(yp, zh)]
        arrived(rows, ("h-", c, None))
        right = rows.at[:, pl.ds(HALF, N - HALF)]
        send(right, right, ("hv-", c), to_ym)
        send(rows, rows, ("hz-", c, None), to_zh)

    def far(c):
        rows = H.at[c, own(y2, zh)]
        arrived(rows.at[:, pl.ds(0, HALF)], ("hv+", c))
        arrived(rows.at[:, pl.ds(HALF, N - HALF)], ("hv-", c))
        send(rows, rows, ("hz2", c, None), to_zh)

    def down_tile(c, n):
        cols = pl.ds(pl.multiple_of(n * 1024, 1024), 1024)
        rows = H[c].reshape(128, N)
        part = jnp.dot(rows, WD[:, cols], preferred_element_type=F32)
        D[c % 2, :, :, cols] = part.reshape(2, 64, 1024)

    def hidden_arrived(c, g):
        keys = [("hz", y, zo), ("hz+", ym, zo), ("hz-", yp, zo), ("hz2", y2, zo)]
        if c in Z_FIRST:
            keys = keys[1:]
        if c in DIRECT + Z_FIRST:
            keys += [("h+", ym, zh), ("h-", yp, zh), ("h2", y2, zh)]
        for key, y_, z_ in keys:
            arrived(H.at[c, own(y_, z_), :, hidden_columns(g)], (key, c, g))

    def before_down(c):
        if c == 0:
            wd_copy.wait()
        if c >= 2:
            on_way.pop(("core", c - 2)).wait_send()

    def down(c):
        hidden_arrived(c, None)
        before_down(c)

        def step(n, carry):
            down_tile(c, n)
            return carry

        lax.fori_loop(0, 2, step, 0)
        send(D.at[c % 2, other], CR.at[c], ("core", c), to_core)

    def down_first(c):
        hidden_arrived(c, 0)
        before_down(c)

        def step(n, carry):
            cols = pl.ds(pl.multiple_of(n * 1024, 1024), 1024)
            rows = H[c, :, :, pl.ds(0, 896)].reshape(128, 896)
            part = jnp.dot(rows, WD[pl.ds(0, 896), cols], preferred_element_type=F32)
            D[c % 2, :, :, cols] = part.reshape(2, 64, 1024)
            return carry

        lax.fori_loop(0, 2, step, 0)

    def down_rest(c, n):
        if n == 0:
            hidden_arrived(c, 1)
        cols = pl.ds(n * 1024, 1024)
        rows = H[c, :, :, pl.ds(896, 768)].reshape(128, 768)
        part = jnp.dot(rows, WD[pl.ds(896, 768), cols], preferred_element_type=F32)
        D[c % 2, :, :, cols] += part.reshape(2, 64, 1024)
        send(D.at[c % 2, other, :, cols], CR.at[c, :, cols], ("core", c, n), to_core)

    def add_cores(c, cols, tag):
        name = CHUNKS[c]
        arrived(CR.at[c, :, cols], ("core", c) + tag)
        total = D[c % 2, core, :, cols] + CR[c, :, cols]
        if name not in ALONG_X:
            ACC[("own", "z").index(name), :, cols] = total
            return
        XS[c, :, cols] = total.astype(BF)
        ways = ALONG_X[name]
        rows = 64 // len(ways)
        for i, d in enumerate(ways):
            part = pl.ds(i * rows, rows)
            send(XS.at[c, part, cols], XR.at[c, part, cols], ("x", c, i) + tag, to_x[d])

    def over_core(c):
        add_cores(c, pl.ds(0, M), ())

    def sums_arrived(c):
        ways = ALONG_X[CHUNKS[c]]
        rows = 64 // len(ways)
        for i in range(len(ways)):
            part = pl.ds(i * rows, rows)
            if c in SPLIT:
                for n in range(2):
                    cols = pl.ds(n * 1024, 1024)
                    arrived(XR.at[c, part, cols], ("x", c, i, n))
            else:
                arrived(XR.at[c, part], ("x", c, i))

    def partner(i):
        whole = CHUNKS.index("zx2")
        half = CHUNKS.index(("zmixA", "zmixB")[i])
        if i == 0:
            sums_arrived(whole)
        sums_arrived(half)
        rows = pl.ds(32 * i, 32)
        total = ACC[1, rows] + XR[whole, rows].astype(F32)
        total = total + XR[half, 0:32].astype(F32) + XR[half, 32:64].astype(F32)
        ZLB[rows] = total.astype(BF)
        send(ZLB.at[rows], ZLR.at[rows], ("z_lo", i), to_zl)

    own_key, z_key = ("fwd", CHUNKS.index("own")), ("tok", "z")
    send(mine, T.at[CHUNKS.index("own"), core], own_key, to_core)
    send(mine, T.at[CHUNKS.index("z"), core], z_key, to_zl)

    steps = {
        SEND_FAR: send_far, SEND_NEAR: send_near, FORWARD: forward, GATE_UP: gate_up, NEAR_SUMS: near_sums,
        RELAY: relay, RELAY_A: lambda c: relay(c, 0), RELAY_B: lambda c: relay(c, 1),
        OVER_Y: over_y, OVER_Y_A: lambda c: over_y(c, 0), OVER_Y_B: lambda c: over_y(c, 1),
        HIDDEN: hidden, HIDDEN_A: lambda c: hidden(c, 0), HIDDEN_B: lambda c: hidden(c, 1),
        NEAR: near, FAR: far, PASS_ON: pass_on, PASS_ON_A: lambda c: pass_on(c, 0), PASS_ON_B: lambda c: pass_on(c, 1),
        DOWN: down, DOWN_FIRST: down_first, DOWN_A: lambda c: down_rest(c, 0), DOWN_B: lambda c: down_rest(c, 1),
        OVER_CORE: over_core,
        OVER_CORE_A: lambda c: add_cores(c, pl.ds(0, 1024), (0,)),
        OVER_CORE_B: lambda c: add_cores(c, pl.ds(1024, 1024), (1,)),
        PARTNER_A: lambda _: partner(0), PARTNER_B: lambda _: partner(1),
    }
    for name, c in ORDER:
        steps[name](c)

    for key in list(on_way):
        if key[0] not in ("x", "z_lo", "core") or (key[0] == "x" and key[1] not in SPLIT):
            on_way.pop(key).wait_send()

    c2, ca, cb = CHUNKS.index("x2"), CHUNKS.index("mixA"), CHUNKS.index("mixB")
    sums_arrived(c2)
    for i, c in enumerate((ca, cb)):
        rows = pl.ds(32 * i, 32)
        arrived(ZLR.at[rows], ("z_lo", i))
        total = ACC[0, rows] + XR[c2, rows].astype(F32) + ZLR[rows].astype(F32)
        sums_arrived(c)
        total = total + XR[c, 0:32].astype(F32) + XR[c, 32:64].astype(F32)
        out[rows, :] = (total * ds[...][None, :]).astype(BF)

    for c in on_way.values():
        c.wait_send()


def on_device(tokens, gate_weight, up_weight, gate_scale, up_scale, down_weight, down_scale):
    hbm, vmem = pl.BlockSpec(memory_space=pl.ANY), pl.BlockSpec(memory_space=pltpu.VMEM)
    return pl.pallas_call(
        body,
        name="gated_layer",
        out_shape=pltpu.VMEM((64, M), BF),
        in_specs=[hbm] * 7,
        out_specs=vmem,
        scratch_shapes=[
            pltpu.VMEM((N,), F32),
            pltpu.VMEM((N,), F32),
            pltpu.VMEM((M,), F32),
            pltpu.VMEM((K, N2), BF),
            pltpu.VMEM((N, M), BF),
            pltpu.VMEM((NC, 2, 64, K), BF),
            pltpu.VMEM((NC, 8, 16, N2), BF),
            pltpu.VMEM((NC, 2, 16, N2), BF),
            pltpu.VMEM((NC, 2, 16, N2), BF),
            pltpu.VMEM((NC, 2, 16, N2), BF),
            pltpu.VMEM((4, 16, N2), BF),
            pltpu.VMEM((NC, 16, N2), BF),
            pltpu.VMEM((NC, 8, 16, N), BF),
            pltpu.VMEM((2, 2, 64, M), F32),
            pltpu.VMEM((NC, 64, M), F32),
            pltpu.VMEM((NC, 64, M), BF),
            pltpu.VMEM((NC, 64, M), BF),
            pltpu.VMEM((2, 64, M), F32),
            pltpu.VMEM((64, M), BF),
            pltpu.VMEM((64, M), BF),
            pltpu.SemaphoreType.DMA((NSEM,)),
            pltpu.SemaphoreType.DMA((NSEM,)),
            pltpu.SemaphoreType.DMA((10,)),
        ],
        compiler_params=pltpu.CompilerParams(
            collective_id=0, has_side_effects=True, vmem_limit_bytes=62 * 2**20
        ),
        cost_estimate=pl.CostEstimate(
            flops=2 * 1024 * K * N2 + 2 * 1024 * N * M, bytes_accessed=2 * (K * N2 + N * M), transcendentals=0
        ),
    )(tokens, gate_weight, up_weight, gate_scale, up_scale, down_weight, down_scale)


def solution(mesh):
    return jax.shard_map(
        on_device,
        mesh=mesh,
        in_specs=(
            P("gy", "gx"),
            P("gx", "gy"),
            P("gx", "gy"),
            P("gy"),
            P("gy"),
            P("gy", "gx"),
            P("gx"),
        ),
        out_specs=P("gy", "gx"),
        check_vma=False,
    )
```
